512 devices in a mesh: xy: 32 (over z_hi, y), gz: 16 (over x, z_lo, core).
Axes of the slice: x: 4, y: 8, z: 8 (z_hi: 4, z_lo: 2; z = z_hi * 2 + z_lo), core: 2. Of those that a mesh axis runs over, the one named last changes fastest.
Arguments:
- volume: float32 [64, 1024, 2048], P('gz', 'xy'), may hold values from -6 to 6
- measured: float32 [4, 1024, 2048], P(None, 'xy'), may hold values from -6 to 6
- ray_offset: int32 [4, 64], replicated, may hold values from -128 to 127, as said below
- defocus: int32 [4, 16], replicated, may hold values from 8000 to 39999
Outputs:
- updated: float32 [64, 1024, 2048], P('gz', 'xy')
The draws below stay inside these ranges and needn't reach their ends.
Inputs may be any that keep to these rules, and one draw needn't show every extreme that they name: `ray_offset`: one tilt has offset -128 at the first layer and 127 at the last.
All inputs are finite; a program needn't handle non-finite values.
Results may differ from the reference program's by a relative error of at most 0.0003.
Values sent between devices are 32-bit elements; how exact they have to be, the bound alone decides.
A program may use at most 64 MiB of HBM per device.

```python
import math
import jax
import jax.numpy as jnp
from jax import lax

NY = 2048
TILTS = 4
HALO = 16
CZ = 4
NX = 1024
NZ = 64
SLABS = 16


def draw_ray_offset(key, part):
    key = jax.random.fold_in(key, 7)
    key_base, key_tilt = jax.random.split(key)
    base = jax.random.randint(key_base, (TILTS, NZ), -8 * HALO, 8 * HALO, dtype=jnp.int32)
    chosen = jax.random.randint(key_tilt, (), 0, TILTS, dtype=jnp.int32)
    tilt_index = jnp.arange(TILTS, dtype=jnp.int32)[:, None]
    layer_index = jnp.arange(NZ, dtype=jnp.int32)[None, :]
    base = jnp.where((tilt_index == chosen) & (layer_index == 0), -8 * HALO, base)
    base = jnp.where((tilt_index == chosen) & (layer_index == NZ - 1), 8 * HALO - 1, base)
    return base.astype(jnp.int32)


def set_ends(drawn, rng, smallest, high):
    index_at = [jax.random.randint(jax.random.fold_in(rng, axis), (), 0, length) for axis, length in enumerate(drawn.shape)]
    widest = drawn.shape.index(max(drawn.shape))
    neighbour = index_at[:widest] + [(index_at[widest] + 1) % drawn.shape[widest]] + index_at[widest + 1:]
    return drawn.at[tuple(index_at)].set(smallest).at[tuple(neighbour)].set(high)


def block_levels(key, dims, shards, smallest, largest):
    loudness, own = 1.0, jax.random.fold_in(key, 6)
    for position, shards_of in shards:
        draws = jnp.exp(jax.random.uniform(jax.random.fold_in(own, position), (shards_of,), jnp.float32, smallest / len(shards), largest / len(shards)))
        loudness = loudness * jnp.repeat(draws, dims[position] // shards_of).reshape([-1 if axis == position else 1 for axis in range(len(dims))])
    return loudness


def gaussian(own_key, dims, deviation, reach, shards=(), held_as=jnp.bfloat16):
    result = deviation * jax.random.normal(own_key, dims, jnp.float32)
    if shards:
        result = result * block_levels(own_key, dims, shards, -0.22, 0.18)
    return jnp.clip(result, -reach, reach).astype(held_as)


def setup_inputs(seed: int = 0) -> dict:
    splits = jax.random.split(jax.random.key(seed), 5)
    volume = gaussian(splits[0], (NZ, NX, NY), 1.0, 6.0, ((0, 16), (1, 32)), jnp.float32)
    measured = gaussian(splits[1], (TILTS, NX, NY), 1.0, 6.0, ((1, 32),), jnp.float32)
    ray_offset = draw_ray_offset(jax.random.fold_in(splits[4], 71), 0)
    defocus = set_ends(jax.random.randint(splits[3], (TILTS, SLABS), 8000, 40000), jax.random.fold_in(splits[3], 1), 8000, 39999).astype(jnp.int32)
    return {"volume": volume, "measured": measured, "ray_offset": ray_offset, "defocus": defocus}


pixel_size = 4.0
wavelength = 0.0197
contrast = 0.07
amplitude_root = math.sqrt(1.0 - 0.07 * 0.07)

def ctf_response(defocus, length):
    index = jnp.arange(length, dtype=jnp.int32)
    frequency = jnp.where(2 * index < length, index, index - length).astype(jnp.float32) / (length * pixel_size)
    phase = math.pi * wavelength * defocus.astype(jnp.float32)[:, :, None] * frequency * frequency
    return -(amplitude_root * jnp.sin(phase) + contrast * jnp.cos(phase))

def reference(volume, measured, ray_offset, defocus):
    shifts = (ray_offset // 8).astype(jnp.int32)
    far_weight = (ray_offset % 8).astype(jnp.float32) / 8.0
    near_weight = 1.0 - far_weight
    padded = jnp.pad(volume, ((0, 0), (HALO, HALO), (0, 0)))

    def project(total, layer):
        plane, shift_row, near_row, far_row = layer

        def take(start):
            return lax.dynamic_slice_in_dim(plane, start, NX, 0)
        near_rows = jax.vmap(take)((shift_row + HALO).astype(jnp.int32))
        far_rows = jax.vmap(take)((shift_row + HALO + 1).astype(jnp.int32))
        return (total + near_row[:, None, None] * near_rows + far_row[:, None, None] * far_rows, None)
    projection = lax.scan(project, jnp.zeros((TILTS, NX, NY), jnp.float32), (padded, shifts.T, near_weight.T, far_weight.T))[0]
    residual = measured - NZ ** (-0.5) * projection
    response = ctf_response(defocus, NY)
    spectrum = jnp.fft.fft(residual, axis=-1)

    def filter_slab(response_slab):
        return jnp.real(jnp.fft.ifft(spectrum * response_slab[:, None, :], axis=-1)).astype(residual.dtype)
    filtered = lax.map(filter_slab, jnp.transpose(response, (1, 0, 2)))

    def spread(carry, layer):
        z_index, shift_row, near_row, far_row = layer
        slab_rows = lax.dynamic_index_in_dim(filtered, z_index // CZ, 0, keepdims=False)
        wide = jnp.pad(slab_rows, ((0, 0), (HALO, HALO), (0, 0)))

        def take(rows_tilt, start):
            return lax.dynamic_slice_in_dim(rows_tilt, start, NX, 0)
        near_rows = jax.vmap(take)(wide, (HALO - shift_row).astype(jnp.int32))
        far_rows = jax.vmap(take)(wide, (HALO - shift_row - 1).astype(jnp.int32))
        layer_sum = lax.optimization_barrier(jnp.sum(near_row[:, None, None] * near_rows + far_row[:, None, None] * far_rows, axis=0))
        return (carry, layer_sum)
    update = lax.scan(spread, jnp.zeros((), jnp.float32), (jnp.arange(NZ, dtype=jnp.int32), shifts.T, near_weight.T, far_weight.T))[1]
    return volume + update / TILTS
```

```python
import functools
import math

import jax
import jax.numpy as jnp
import ml_dtypes
import numpy as np
from jax import lax
from jax.experimental import pallas as pl
from jax.experimental.pallas import tpu as pltpu
from jax.sharding import PartitionSpec as P

HALO = 16
LINE = 2048
PART = 256
ROWS = 32
LAYERS = 4
TILTS = 4

pixel_size = 4.0
wavelength = 0.0197
contrast = 0.07
amplitude_root = math.sqrt(1.0 - 0.07 * 0.07)
f32 = jnp.float32
bf16 = jnp.bfloat16
MESH = pl.DeviceIdType.MESH

GROUPS = ((0, 256, 0), (256, 256, 4), (512, 512, 1), (1024, 512, 2), (1536, 512, 3))


def halves(table):
    high = table.astype(ml_dtypes.bfloat16)
    low = (table - high.astype(np.float64)).astype(ml_dtypes.bfloat16)
    return np.stack([high, low])


def dft_tables():
    b = np.arange(PART, dtype=np.int64)[:, None]
    tables, freq, scale = {}, [], []
    for _, width, residue in GROUPS:
        if residue == 0:
            re, im = np.arange(0, 129), np.arange(1, 128)
        elif residue == 4:
            re = im = np.arange(0, 128)
        else:
            re = im = np.arange(0, 256)
        f_re, f_im = residue + 8 * re, residue + 8 * im
        turn_re = 2 * np.pi / LINE * (b * f_re % LINE)
        turn_im = 2 * np.pi / LINE * (b * f_im % LINE)
        real_in = np.concatenate([np.cos(turn_re), -np.sin(turn_im)], 1)
        if width == 512:
            imag_in = np.concatenate([np.sin(turn_re), np.cos(turn_im)], 1)
            real_in = np.concatenate([real_in, imag_in], 0)
        tables[residue] = real_in
        f = np.concatenate([f_re, f_im])
        folded = np.where(2 * f < LINE, f, f - LINE)
        freq.append(folded / (LINE * pixel_size))
        scale.append(np.where((f == 0) | (f == LINE // 2), 1.0, 2.0) / (LINE * TILTS))
    big = np.stack([tables[1], tables[2], tables[3]])
    small = np.stack([tables[0], tables[4]])
    line = np.stack([np.concatenate(freq), np.concatenate(scale)]).astype(np.float32)
    return (
        halves(big),
        halves(small),
        halves(big.transpose(0, 2, 1)),
        halves(small.transpose(0, 2, 1)),
        line,
    )


def split(x):
    high = x.astype(bf16)
    low = (x - high.astype(f32)).astype(bf16)
    return high, low


def dot(a, b):
    return jnp.dot(a, b, preferred_element_type=f32)


def kernel(
    tiles,
    ray,
    defocus,
    vol,
    meas,
    line,
    fwd_big_hbm,
    fwd_small_hbm,
    inv_big_hbm,
    inv_small_hbm,
    out,
    fwd_big,
    fwd_small,
    inv_big,
    inv_small,
    meas_own,
    vcat,
    other_g,
    other_o,
    mine_g,
    mine_o,
    core_g,
    core_o,
    relay_g,
    fin_g,
    zin_g,
    zin_o,
    relay_o,
    fin_o,
    halo_in,
    gathered,
    spectral,
    local_sem,
    ss,
    rs,
):
    gz = lax.axis_index("gz")
    xy = lax.axis_index("xy")
    X = gz // 4
    zl = (gz // 2) % 2
    c = gz % 2
    to_core = {"gz": gz + 1 - 2 * c}
    to_z = {"gz": gz + 2 - 4 * zl}
    to_right = {"gz": (gz + 4) % 16}
    to_left = {"gz": (gz + 12) % 16}
    step = 1 - 2 * zl
    to_ahead = {"xy": (xy + step + tiles) % tiles}
    to_behind = {"xy": (xy - step + tiles) % tiles}
    partners = (to_core, to_z, to_right, to_left, to_ahead, to_behind)
    barrier = pltpu.get_barrier_semaphore()
    for partner in partners:
        pl.semaphore_signal(barrier, inc=1, device_id=partner, device_id_type=MESH)

    k_own = zl * 2 + c
    locals_ = [
        pltpu.make_async_copy(meas.at[X, pl.ds(pl.multiple_of(8 * k_own, 8), 8)], meas_own, local_sem.at[0]),
        pltpu.make_async_copy(fwd_big_hbm, fwd_big, local_sem.at[1]),
        pltpu.make_async_copy(fwd_small_hbm, fwd_small, local_sem.at[2]),
        pltpu.make_async_copy(inv_big_hbm, inv_big, local_sem.at[3]),
        pltpu.make_async_copy(inv_small_hbm, inv_small, local_sem.at[4]),
    ]
    for copy in locals_:
        copy.start()

    count = [0]
    sent = []

    def send(src, dst, where):
        i = count[0]
        count[0] += 1
        copy = pltpu.make_async_remote_copy(
            src_ref=src, dst_ref=dst, send_sem=ss.at[i], recv_sem=rs.at[i],
            device_id=where, device_id_type=MESH,
        )
        copy.start()
        sent.append(copy)
        return copy

    shift, far = {}, {}
    for dt in range(4):
        t = (X + dt) % 4
        for z in range(LAYERS):
            offset = ray[t, gz * LAYERS + z]
            shift[dt, z] = offset >> 3
            far[dt, z] = (offset & 7).astype(f32) * 0.125

    col = lax.broadcasted_iota(jnp.int32, (8, 128), 1)
    sub = lax.broadcasted_iota(jnp.int32, (8, 128), 0)
    layer = col // ROWS
    target, near_row, far_row = {}, {}, {}
    for dt in range(4):
        s = jnp.zeros((8, 128), jnp.int32)
        w = jnp.zeros((8, 128), f32)
        for z in range(LAYERS):
            s = jnp.where(layer == z, shift[dt, z], s)
            w = jnp.where(layer == z, far[dt, z], w)
        target[dt] = col % ROWS - s
        near_row[dt], far_row[dt] = 1.0 - w, w

    def first_ext(zone, core, ghost):
        base = 8 * (zone * 2 + core)
        if ghost:
            base = base + 32 - 64 * zone
        return base

    def weights(core, ghost, dt, dzl):
        zone = zl ^ dzl
        e = sub + first_ext(zone, core, ghost)
        return jnp.where(e == target[dt], near_row[dt], 0.0) + jnp.where(
            e == target[dt] - 1, far_row[dt], 0.0
        )

    def lhs(core):
        blocks = [weights(core, True, dt, dzl) for dt in range(4) for dzl in range(2)]
        blocks += [weights(core, False, dt, dzl) for dzl in range(2) for dt in range(4)]
        w = jnp.concatenate(blocks, 0).astype(bf16)
        return jnp.concatenate([w, w], 1)

    volume = vol[...].reshape(LAYERS * ROWS, LINE)
    vh, vl = split(volume)
    vcat[0:128, :] = vh
    vcat[128:256, :] = vl

    def project(core, to_g, to_o):
        w = lhs(core)
        for j in range(4):
            at = pl.ds(512 * j, 512)
            p = dot(w, vcat[:, at])
            to_g[:, :, :, at] = p[0:64].reshape(4, 2, 8, 512)
            to_o[:, :, :, at] = p[64:128].reshape(2, 4, 8, 512)

    project(1 - c, other_g, other_o)
    pl.semaphore_wait(barrier, len(partners))
    cg, co = {}, {}
    cg[2] = send(other_g.at[2], core_g.at[2], to_core)
    co[1] = send(other_o.at[1], core_o.at[1], to_core)
    cg[1] = send(other_g.at[1], core_g.at[1], to_core)
    cg[3] = send(other_g.at[3], core_g.at[3], to_core)
    co[0] = send(other_o.at[0], core_o.at[0], to_core)
    cg[0] = send(other_g.at[0], core_g.at[0], to_core)
    project(c, mine_g, mine_o)

    def add(dst, src):
        dst[...] = dst[...] + src[...]

    half = (pl.ds(0, 1024), pl.ds(1024, 1024))
    cg[2].wait_recv()
    add(mine_g.at[2], core_g.at[2])
    g_relay_right = send(mine_g.at[2, 0], relay_g.at[0], to_right)
    g_relay_left = send(mine_g.at[2, 1], relay_g.at[1], to_left)
    co[1].wait_recv()
    add(mine_o.at[1], core_o.at[1])
    oz = {}
    for dt in (2, 1, 3, 0):
        oz[dt] = send(mine_o.at[1, dt], zin_o.at[dt], to_z)
    cg[1].wait_recv()
    add(mine_g.at[1], core_g.at[1])
    g_plain_right = send(mine_g.at[1, 1], fin_g.at[0, 1], to_right)
    cg[3].wait_recv()
    add(mine_g.at[3], core_g.at[3])
    g_plain_left = send(mine_g.at[3, 0], fin_g.at[1, 0], to_left)
    co[0].wait_recv()
    add(mine_o.at[0], core_o.at[0])
    cg[0].wait_recv()
    add(mine_g.at[0], core_g.at[0])

    g_relay_right.wait_recv()
    add(mine_g.at[1, 0], relay_g.at[0])
    g_fin_right = send(mine_g.at[1, 0], fin_g.at[0, 0], to_right)
    g_relay_left.wait_recv()
    add(mine_g.at[3, 1], relay_g.at[1])
    g_fin_left = send(mine_g.at[3, 1], fin_g.at[1, 1], to_left)

    oz[2].wait_recv()
    add(mine_o.at[0, 2], zin_o.at[2])
    o_relay_right = send(mine_o.at[0, 2, :, half[0]], relay_o.at[0], to_right)
    o_relay_left = send(mine_o.at[0, 2, :, half[1]], relay_o.at[1], to_left)
    oz[1].wait_recv()
    add(mine_o.at[0, 1], zin_o.at[1])
    o_plain_right = send(mine_o.at[0, 1, :, half[1]], fin_o.at[0, :, half[1]], to_right)
    oz[3].wait_recv()
    add(mine_o.at[0, 3], zin_o.at[3])
    o_plain_left = send(mine_o.at[0, 3, :, half[0]], fin_o.at[1, :, half[0]], to_left)

    g_plain_right.wait_recv()
    g_plain_left.wait_recv()
    g_fin_right.wait_recv()
    g_fin_left.wait_recv()
    mine_g[0] = mine_g[0] + fin_g[0] + fin_g[1]
    gz_copy = send(mine_g.at[0, 1], zin_g, to_z)

    o_relay_right.wait_recv()
    add(mine_o.at[0, 1, :, half[0]], relay_o.at[0])
    o_fin_right = send(mine_o.at[0, 1, :, half[0]], fin_o.at[0, :, half[0]], to_right)
    o_relay_left.wait_recv()
    add(mine_o.at[0, 3, :, half[1]], relay_o.at[1])
    o_fin_left = send(mine_o.at[0, 3, :, half[1]], fin_o.at[1, :, half[1]], to_left)

    gz_copy.wait_recv()
    add(mine_g.at[0, 0], zin_g)
    halo = send(mine_g.at[0, 0], halo_in, to_ahead)

    oz[0].wait_recv()
    o_plain_right.wait_recv()
    o_plain_left.wait_recv()
    o_fin_right.wait_recv()
    o_fin_left.wait_recv()
    total = mine_o[0, 0] + zin_o[0] + fin_o[0] + fin_o[1]
    for copy in locals_:
        copy.wait()
    halo.wait_recv()
    behind = xy - step
    inside = (behind >= 0) & (behind < tiles)
    total = total + jnp.where(inside, halo_in[...], 0.0)
    ray_norm = float(TILTS * 16) ** (-0.5)
    residual = meas_own[...] - ray_norm * total

    x = [residual[:, PART * a : PART * (a + 1)] for a in range(8)]
    root = math.sqrt(0.5)
    s04, d04 = x[0] + x[4], x[0] - x[4]
    s26, d26 = x[2] + x[6], x[2] - x[6]
    s15, d15 = x[1] + x[5], x[1] - x[5]
    s37, d37 = x[3] + x[7], x[3] - x[7]
    even, odd = s04 + s26, s15 + s37
    m = root * (d15 - d37)
    n = root * (d15 + d37)
    inputs = {
        0: even + odd,
        4: even - odd,
        1: jnp.concatenate([d04 + m, -(d26 + n)], 1),
        2: jnp.concatenate([s04 - s26, s37 - s15], 1),
        3: jnp.concatenate([d04 - m, d26 - n], 1),
    }
    for first, width, residue in GROUPS:
        high, low = split(inputs[residue])
        if width == 512:
            th, tl = fwd_big[0, residue - 1], fwd_big[1, residue - 1]
        else:
            th, tl = fwd_small[0, residue // 4], fwd_small[1, residue // 4]
        both = dot(jnp.concatenate([high, low], 0), th)
        gathered[0, 0, 0, 0, :, first : first + width] = both[0:8] + both[8:16] + dot(high, tl)

    own = gathered.at[0, 0, 0, 0]
    a_halo = send(own, gathered.at[0, 0, 0, 1], to_behind)
    ar = send(own, gathered.at[0, 3, 0, 0], to_right)
    al = send(own, gathered.at[0, 1, 0, 0], to_left)
    az = {0: [send(own, gathered.at[0, 0, 1, 0], to_z)]}
    cores = []

    def to_other(dt, dzl, ghost):
        cores.append(send(gathered.at[0, dt, dzl, ghost], gathered.at[1, dt, dzl, ghost], to_core))

    to_other(0, 0, 0)
    ar.wait_recv()
    arr = send(gathered.at[0, 3, 0, 0, :, half[0]], gathered.at[0, 2, 0, 0, :, half[0]], to_right)
    az[3] = [send(gathered.at[0, 3, 0, 0], gathered.at[0, 3, 1, 0], to_z)]
    al.wait_recv()
    arl = send(gathered.at[0, 1, 0, 0, :, half[1]], gathered.at[0, 2, 0, 0, :, half[1]], to_left)
    az[1] = [send(gathered.at[0, 1, 0, 0], gathered.at[0, 1, 1, 0], to_z)]
    a_halo.wait_recv()
    gzc = send(gathered.at[0, 0, 0, 1], gathered.at[0, 0, 1, 1], to_z)
    gr0 = send(gathered.at[0, 0, 0, 1], gathered.at[0, 3, 0, 1], to_right)
    gl0 = send(gathered.at[0, 0, 0, 1], gathered.at[0, 1, 0, 1], to_left)
    to_other(3, 0, 0)
    to_other(1, 0, 0)
    to_other(0, 0, 1)
    arr.wait_recv()
    arl.wait_recv()
    az[2] = [send(gathered.at[0, 2, 0, 0], gathered.at[0, 2, 1, 0], to_z)]
    to_other(2, 0, 0)
    gzc.wait_recv()
    gr1 = send(gathered.at[0, 0, 1, 1], gathered.at[0, 3, 1, 1], to_right)
    gl1 = send(gathered.at[0, 0, 1, 1], gathered.at[0, 1, 1, 1], to_left)
    to_other(0, 1, 1)
    az[0][0].wait_recv()
    to_other(0, 1, 0)
    gr0.wait_recv()
    grr = send(gathered.at[0, 3, 0, 1], gathered.at[0, 2, 0, 1], to_right)
    to_other(3, 0, 1)
    gl0.wait_recv()
    to_other(1, 0, 1)
    gl1.wait_recv()
    grl = send(gathered.at[0, 1, 1, 1], gathered.at[0, 2, 1, 1], to_left)
    to_other(1, 1, 1)
    gr1.wait_recv()
    to_other(3, 1, 1)
    az[3][0].wait_recv()
    to_other(3, 1, 0)
    az[1][0].wait_recv()
    to_other(1, 1, 0)

    frequency = line[0:1, :]
    ctf = []
    for dt in range(4):
        number = defocus[(X + dt) % 4, gz].astype(f32)
        phase = math.pi * wavelength * number * frequency * frequency
        ctf.append(
            -(amplitude_root * jnp.sin(phase) + contrast * jnp.cos(phase)) * line[1:2, :]
        )

    gcol = lax.broadcasted_iota(jnp.int32, (ROWS, 256), 1)
    grow = lax.broadcasted_iota(jnp.int32, (ROWS, 256), 0)
    zone = zl ^ ((gcol >> 4) & 1)
    place = 8 * (zone * 2 + (c ^ (gcol >> 7))) + (gcol & 7)
    place = place + ((gcol >> 3) & 1) * (32 - 64 * zone)
    tilt = (gcol >> 5) & 3
    there = place + xy * ROWS
    legal = (there >= 0) & (there < tiles * ROWS)
    back = []
    for z in range(LAYERS):
        s = jnp.zeros((ROWS, 256), jnp.int32)
        w = jnp.zeros((ROWS, 256), f32)
        for dt in range(4):
            s = jnp.where(tilt == dt, shift[dt, z], s)
            w = jnp.where(tilt == dt, far[dt, z], w)
        delta = place + s - grow
        both = jnp.where(delta == 0, 1.0 - w, 0.0) + jnp.where(delta == -1, w, 0.0)
        back.append(jnp.where(legal, both, 0.0))
    back = jnp.concatenate(back, 0).astype(bf16)

    az[2][0].wait_recv()
    to_other(2, 1, 0)
    grr.wait_recv()
    to_other(2, 0, 1)
    grl.wait_recv()
    to_other(2, 1, 1)
    for copy in cores:
        copy.wait_recv()

    for first, width, residue in GROUPS:
        at = pl.ds(first, width)
        highs, lows = [], []
        for dc in range(2):
            for dt in range(4):
                block = gathered[dc, dt, :, :, :, at].reshape(32, width)
                high, low = split(block * ctf[dt][:, first : first + width])
                highs.append(high)
                lows.append(low)
        u = dot(back, jnp.concatenate(highs, 0)) + dot(back, jnp.concatenate(lows, 0))
        high, low = split(u)
        if width == 512:
            th, tl = inv_big[0, residue - 1], inv_big[1, residue - 1]
        else:
            th, tl = inv_small[0, residue // 4], inv_small[1, residue // 4]
        spectral[:, at] = dot(high, th) + dot(low, th) + dot(high, tl)

    def part(first):
        return spectral[:, first : first + PART]

    g0, g4 = part(0), part(256)
    r1, i1, r2, i2, r3, i3 = (part(512 + PART * i) for i in range(6))
    p, q = g0 + g4, g0 - g4
    pr, ps = p + r2, p - r2
    qm, qp = q - i2, q + i2
    r13, i31 = r1 + r3, i3 - i1
    rd, im = r1 - r3, i1 + i3
    v, w = root * (rd - im), root * (rd + im)
    ys = (pr + r13, qm + v, ps + i31, qp - w, pr - r13, qm - v, ps - i31, qp + w)
    for a in range(8):
        at = pl.ds(PART * a, PART)
        out[:, :, at] = vol[:, :, at] + ys[a].reshape(LAYERS, ROWS, PART)

    for copy in sent:
        copy.wait_send()


def body(tiles, tables, volume, measured, ray_offset, defocus):
    fwd_big, fwd_small, inv_big, inv_small, line = tables
    vmem = pl.BlockSpec(memory_space=pltpu.VMEM)
    smem = pl.BlockSpec(memory_space=pltpu.SMEM)
    anywhere = pl.BlockSpec(memory_space=pl.ANY)

    def f(*shape):
        return pltpu.VMEM(shape, f32)

    return pl.pallas_call(
        functools.partial(kernel, tiles),
        out_shape=jax.ShapeDtypeStruct(volume.shape, f32),
        in_specs=[smem, smem, vmem, anywhere, vmem, anywhere, anywhere, anywhere, anywhere],
        out_specs=vmem,
        scratch_shapes=[
            pltpu.VMEM(fwd_big.shape, bf16),
            pltpu.VMEM(fwd_small.shape, bf16),
            pltpu.VMEM(inv_big.shape, bf16),
            pltpu.VMEM(inv_small.shape, bf16),
            f(8, LINE),
            pltpu.VMEM((256, LINE), bf16),
            f(4, 2, 8, LINE),
            f(2, 4, 8, LINE),
            f(4, 2, 8, LINE),
            f(2, 4, 8, LINE),
            f(4, 2, 8, LINE),
            f(2, 4, 8, LINE),
            f(2, 8, LINE),
            f(2, 2, 8, LINE),
            f(8, LINE),
            f(4, 8, LINE),
            f(2, 8, LINE // 2),
            f(2, 8, LINE),
            f(8, LINE),
            f(2, 4, 2, 2, 8, LINE),
            f(128, LINE),
            pltpu.SemaphoreType.DMA((5,)),
            pltpu.SemaphoreType.DMA((64,)),
            pltpu.SemaphoreType.DMA((64,)),
        ],
        compiler_params=pltpu.CompilerParams(
            collective_id=0, has_side_effects=True, vmem_limit_bytes=48 * 1024 * 1024
        ),
        name="step",
    )(ray_offset, defocus, volume, measured, line, fwd_big, fwd_small, inv_big, inv_small)


def solution(mesh):
    placed = (P("gz", "xy", None), P(None, "xy", None), P(), P())
    tables = tuple(dft_tables())
    return jax.shard_map(
        functools.partial(body, mesh.shape["xy"], tables),
        mesh=mesh,
        in_specs=placed,
        out_specs=P("gz", "xy", None),
        check_vma=False,
    )
```

```python
import functools
import math

import jax
import jax.numpy as jnp
import ml_dtypes
import numpy as np
from jax import lax
from jax.experimental import pallas as pl
from jax.experimental.pallas import tpu as pltpu
from jax.sharding import PartitionSpec as P

HALO = 16
LINE = 2048
PART = 256
ROWS = 32
LAYERS = 4
TILTS = 4

pixel_size = 4.0
wavelength = 0.0197
contrast = 0.07
amplitude_root = math.sqrt(1.0 - 0.07 * 0.07)
f32 = jnp.float32
bf16 = jnp.bfloat16
MESH = pl.DeviceIdType.MESH

GROUPS = ((0, 256, 0), (256, 256, 4), (512, 512, 1), (1024, 512, 2), (1536, 512, 3))


def halves(table):
    high = table.astype(ml_dtypes.bfloat16)
    low = (table - high.astype(np.float64)).astype(ml_dtypes.bfloat16)
    return np.stack([high, low])


def dft_tables():
    b = np.arange(PART, dtype=np.int64)[:, None]
    tables, freq, scale = {}, [], []
    for _, width, residue in GROUPS:
        if residue == 0:
            re, im = np.arange(0, 129), np.arange(1, 128)
        elif residue == 4:
            re = im = np.arange(0, 128)
        else:
            re = im = np.arange(0, 256)
        f_re, f_im = residue + 8 * re, residue + 8 * im
        turn_re = 2 * np.pi / LINE * (b * f_re % LINE)
        turn_im = 2 * np.pi / LINE * (b * f_im % LINE)
        real_in = np.concatenate([np.cos(turn_re), -np.sin(turn_im)], 1)
        if width == 512:
            imag_in = np.concatenate([np.sin(turn_re), np.cos(turn_im)], 1)
            real_in = np.concatenate([real_in, imag_in], 0)
        tables[residue] = real_in
        f = np.concatenate([f_re, f_im])
        folded = np.where(2 * f < LINE, f, f - LINE)
        freq.append(folded / (LINE * pixel_size))
        scale.append(np.where((f == 0) | (f == LINE // 2), 1.0, 2.0) / (LINE * TILTS))
    big = np.stack([tables[1], tables[2], tables[3]])
    small = np.stack([tables[0], tables[4]])
    line = np.stack([np.concatenate(freq), np.concatenate(scale)]).astype(np.float32)
    return (
        halves(big),
        halves(small),
        halves(big.transpose(0, 2, 1)),
        halves(small.transpose(0, 2, 1)),
        line,
    )


def split(x):
    high = x.astype(bf16)
    low = (x - high.astype(f32)).astype(bf16)
    return high, low


def dot(a, b):
    return jnp.dot(a, b, preferred_element_type=f32)


def kernel(
    tiles,
    ray_hbm,
    defocus_hbm,
    vol_hbm,
    meas,
    line_hbm,
    fwd_big_hbm,
    fwd_small_hbm,
    inv_big_hbm,
    inv_small_hbm,
    out,
    ray,
    defocus,
    vol,
    line,
    response,
    back_rows,
    fwd_big,
    fwd_small,
    inv_big,
    inv_small,
    meas_rows,
    vcat,
    other_g,
    other_o,
    mine_g,
    mine_o,
    core_g,
    core_o,
    fin_g,
    zin_g,
    zin_o,
    fin_o,
    halo_g,
    halo_o,
    gathered,
    spectral,
    local_sem,
    ss,
    rs,
):
    gz = lax.axis_index("gz")
    xy = lax.axis_index("xy")
    X = gz // 4
    zl = (gz // 2) % 2
    c = gz % 2
    to_core = {"gz": gz + 1 - 2 * c}
    to_z = {"gz": gz + 2 - 4 * zl}
    to_right = {"gz": (gz + 4) % 16}
    to_left = {"gz": (gz + 12) % 16}
    to_far = {"gz": (gz + 8) % 16}
    step = 1 - 2 * zl
    has_ahead = (xy + step >= 0) & (xy + step < tiles)
    has_behind = (xy - step >= 0) & (xy - step < tiles)
    to_ahead = {"xy": (xy + step + tiles) % tiles}
    to_behind = {"xy": (xy - step + tiles) % tiles}
    partners = (to_core, to_z, to_right, to_left, to_far)
    barrier = pltpu.get_barrier_semaphore()

    def greet(partner):
        pl.semaphore_signal(barrier, inc=1, device_id=partner, device_id_type=MESH)

    for partner in partners:
        greet(partner)
    pl.when(has_ahead)(lambda: greet(to_ahead))
    pl.when(has_behind)(lambda: greet(to_behind))
    greetings = len(partners) + has_ahead.astype(jnp.int32) + has_behind.astype(jnp.int32)

    k_own = zl * 2 + c
    meas_hbm = meas.at[X, pl.ds(pl.multiple_of(8 * k_own, 8), 8)]
    start_copies = [
        pltpu.make_async_copy(ray_hbm, ray, local_sem.at[5]),
        pltpu.make_async_copy(vol_hbm, vol, local_sem.at[6]),
    ]
    for copy in start_copies:
        copy.start()

    @pl.when(jnp.logical_not(has_behind))
    def _():
        halo_g[...] = jnp.zeros_like(halo_g)

    @pl.when(jnp.logical_not(has_ahead))
    def _():
        halo_o[...] = jnp.zeros_like(halo_o)
        meas_rows[1] = jnp.zeros((8, LINE), f32)

    locals_ = [
        pltpu.make_async_copy(defocus_hbm, defocus, local_sem.at[7]),
        pltpu.make_async_copy(line_hbm, line, local_sem.at[8]),
        pltpu.make_async_copy(meas_hbm, meas_rows.at[0], local_sem.at[0]),
        pltpu.make_async_copy(fwd_big_hbm, fwd_big, local_sem.at[1]),
        pltpu.make_async_copy(fwd_small_hbm, fwd_small, local_sem.at[2]),
        pltpu.make_async_copy(inv_big_hbm, inv_big, local_sem.at[3]),
        pltpu.make_async_copy(inv_small_hbm, inv_small, local_sem.at[4]),
    ]
    for copy in locals_:
        copy.start()

    count = [0]
    sent = []
    halos = []

    def send(src, dst, where):
        i = count[0]
        count[0] += 1
        copy = pltpu.make_async_remote_copy(
            src_ref=src, dst_ref=dst, send_sem=ss.at[i], recv_sem=rs.at[i],
            device_id=where, device_id_type=MESH,
        )
        copy.start()
        sent.append(copy)
        return copy

    start_copies[0].wait()
    def send_halo(src, dst, where, there, back):
        i = count[0]
        count[0] += 1
        copy = pltpu.make_async_remote_copy(
            src_ref=src, dst_ref=dst, send_sem=ss.at[i], recv_sem=rs.at[i],
            device_id=where, device_id_type=MESH,
        )
        pl.when(there)(copy.start)
        halos.append((copy, there))
        return lambda: pl.when(back)(copy.wait_recv)

    shift, far = {}, {}
    for dt in range(4):
        t = (X + dt) % 4
        for z in range(LAYERS):
            offset = ray[t, gz * LAYERS + z]
            shift[dt, z] = offset >> 3
            far[dt, z] = (offset & 7).astype(f32) * 0.125

    col = lax.broadcasted_iota(jnp.int32, (8, 128), 1)
    sub = lax.broadcasted_iota(jnp.int32, (8, 128), 0)
    layer = col // ROWS
    target, near_row, far_row = {}, {}, {}
    for dt in range(4):
        s = jnp.zeros((8, 128), jnp.int32)
        w = jnp.zeros((8, 128), f32)
        for z in range(LAYERS):
            s = jnp.where(layer == z, shift[dt, z], s)
            w = jnp.where(layer == z, far[dt, z], w)
        target[dt] = col % ROWS - s
        near_row[dt], far_row[dt] = 1.0 - w, w

    def first_ext(zone, core, ghost):
        base = 8 * (zone * 2 + core)
        if ghost:
            base = base + 32 - 64 * zone
        return base

    def weights(core, ghost, dt, dzl):
        zone = zl ^ dzl
        e = sub + first_ext(zone, core, ghost)
        return jnp.where(e == target[dt], near_row[dt], 0.0) + jnp.where(
            e == target[dt] - 1, far_row[dt], 0.0
        )

    def lhs(core):
        blocks = [weights(core, True, dt, dzl) for dt in range(4) for dzl in range(2)]
        blocks += [weights(core, False, dt, dzl) for dzl in range(2) for dt in range(4)]
        w = jnp.concatenate(blocks, 0).astype(bf16)
        return jnp.concatenate([w, w], 1)

    start_copies[1].wait()
    volume = vol[...].reshape(LAYERS * ROWS, LINE)
    vh, vl = split(volume)
    vcat[0:128, :] = vh
    vcat[128:256, :] = vl

    def project(core, to_g, to_o):
        w = lhs(core)
        for j in range(4):
            at = pl.ds(512 * j, 512)
            p = dot(w, vcat[:, at])
            to_g[:, :, :, at] = p[0:64].reshape(4, 2, 8, 512)
            to_o[:, :, :, at] = p[64:128].reshape(2, 4, 8, 512)

    project(1 - c, other_g, other_o)
    pl.semaphore_wait(barrier, greetings)
    cg, co = {}, {}
    cg[2] = send(other_g.at[2], core_g.at[2], to_core)
    co[1] = send(other_o.at[1], core_o.at[1], to_core)
    cg[1] = send(other_g.at[1], core_g.at[1], to_core)
    cg[3] = send(other_g.at[3], core_g.at[3], to_core)
    co[0] = send(other_o.at[0], core_o.at[0], to_core)
    cg[0] = send(other_g.at[0], core_g.at[0], to_core)
    meas_wait = send_halo(meas_hbm, meas_rows.at[1], to_behind, has_behind, has_ahead)
    project(c, mine_g, mine_o)

    for copy in locals_[:2]:
        copy.wait()
    tilt_row = lax.broadcasted_iota(jnp.int32, (TILTS, 1), 0)
    number = jnp.zeros((TILTS, 1), f32)
    for dt in range(4):
        number = jnp.where(tilt_row == dt, defocus[(X + dt) % 4, gz].astype(f32), number)
    frequency = line[0:1, :]
    phase = math.pi * wavelength * number * frequency * frequency
    response[...] = (
        -(amplitude_root * jnp.sin(phase) + contrast * jnp.cos(phase)) * line[1:2, :]
    )

    gcol = lax.broadcasted_iota(jnp.int32, (ROWS, 256), 1)
    grow = lax.broadcasted_iota(jnp.int32, (ROWS, 256), 0)
    zone = zl ^ ((gcol >> 4) & 1)
    place = 8 * (zone * 2 + (c ^ (gcol >> 7))) + (gcol & 7)
    place = place + ((gcol >> 3) & 1) * (32 - 64 * zone)
    tilt = (gcol >> 5) & 3
    there = place + xy * ROWS
    legal = (there >= 0) & (there < tiles * ROWS)
    back = []
    for z in range(LAYERS):
        s = jnp.zeros((ROWS, 256), jnp.int32)
        w = jnp.zeros((ROWS, 256), f32)
        for dt in range(4):
            s = jnp.where(tilt == dt, shift[dt, z], s)
            w = jnp.where(tilt == dt, far[dt, z], w)
        delta = place + s - grow
        both = jnp.where(delta == 0, 1.0 - w, 0.0) + jnp.where(delta == -1, w, 0.0)
        back.append(jnp.where(legal, both, 0.0))
    back_rows[...] = jnp.concatenate(back, 0).astype(bf16)

    def add(dst, src):
        dst[...] = dst[...] + src[...]

    cg[2].wait_recv()
    add(mine_g.at[2], core_g.at[2])
    g_far = send(mine_g.at[2], fin_g.at[2], to_far)
    co[1].wait_recv()
    add(mine_o.at[1], core_o.at[1])
    oz = {}
    for dt in (2, 1, 3, 0):
        oz[dt] = send(mine_o.at[1, dt], zin_o.at[dt], to_z)
    cg[1].wait_recv()
    add(mine_g.at[1], core_g.at[1])
    g_right = send(mine_g.at[1], fin_g.at[0], to_right)
    cg[3].wait_recv()
    add(mine_g.at[3], core_g.at[3])
    g_left = send(mine_g.at[3], fin_g.at[1], to_left)
    co[0].wait_recv()
    add(mine_o.at[0], core_o.at[0])
    cg[0].wait_recv()
    add(mine_g.at[0], core_g.at[0])

    oz[2].wait_recv()
    add(mine_o.at[0, 2], zin_o.at[2])
    o_far = send(mine_o.at[0, 2], fin_o.at[2], to_far)
    oz[1].wait_recv()
    add(mine_o.at[0, 1], zin_o.at[1])
    o_right = send(mine_o.at[0, 1], fin_o.at[0], to_right)
    oz[3].wait_recv()
    add(mine_o.at[0, 3], zin_o.at[3])
    o_left = send(mine_o.at[0, 3], fin_o.at[1], to_left)

    g_far.wait_recv()
    g_right.wait_recv()
    g_left.wait_recv()
    mine_g[0] = (mine_g[0] + fin_g[0]) + (fin_g[1] + fin_g[2])
    g_z = send(mine_g.at[0, 1], zin_g, to_z)

    oz[0].wait_recv()
    o_far.wait_recv()
    o_right.wait_recv()
    o_left.wait_recv()
    mine_o[0, 0] = (mine_o[0, 0] + zin_o[0]) + (fin_o[0] + fin_o[1]) + fin_o[2]
    o_wait = send_halo(mine_o.at[0, 0], halo_o, to_behind, has_behind, has_ahead)
    g_z.wait_recv()
    add(mine_g.at[0, 0], zin_g)
    g_wait = send_halo(mine_g.at[0, 0], halo_g, to_ahead, has_ahead, has_behind)
    for copy in locals_[2:]:
        copy.wait()

    g_wait()
    o_wait()
    meas_wait()
    ray_norm = float(TILTS * 16) ** (-0.5)
    own_sum = mine_o[0, 0] + jnp.where(has_behind, halo_g[...], 0.0)
    own_rows = meas_rows[0] - ray_norm * own_sum
    ghost_rows = meas_rows[1] - ray_norm * (mine_g[0, 0] + halo_o[...])
    ghost_rows = jnp.where(has_ahead, ghost_rows, 0.0)
    residual = jnp.concatenate([own_rows, ghost_rows], 0)

    x = [residual[:, PART * a : PART * (a + 1)] for a in range(8)]
    root = math.sqrt(0.5)
    s04, d04 = x[0] + x[4], x[0] - x[4]
    s26, d26 = x[2] + x[6], x[2] - x[6]
    s15, d15 = x[1] + x[5], x[1] - x[5]
    s37, d37 = x[3] + x[7], x[3] - x[7]
    even, odd = s04 + s26, s15 + s37
    m = root * (d15 - d37)
    n = root * (d15 + d37)
    inputs = {
        0: even + odd,
        4: even - odd,
        1: jnp.concatenate([d04 + m, -(d26 + n)], 1),
        2: jnp.concatenate([s04 - s26, s37 - s15], 1),
        3: jnp.concatenate([d04 - m, d26 - n], 1),
    }
    for first, width, residue in GROUPS:
        high, low = split(inputs[residue])
        if width == 512:
            th, tl = fwd_big[0, residue - 1], fwd_big[1, residue - 1]
        else:
            th, tl = fwd_small[0, residue // 4], fwd_small[1, residue // 4]
        both = dot(jnp.concatenate([high, low], 0), th)
        lines = both[0:16] + both[16:32] + dot(high, tl)
        gathered[0, 0, 0, :, :, first : first + width] = lines.reshape(2, 8, width)

    def block(dt, dzl, ghost):
        return gathered.at[0, dt, dzl, ghost]

    def along_x(dzl, ghost):
        src = block(0, dzl, ghost)
        far = send(src, block(2, dzl, ghost), to_far)
        right = send(src, block(3, dzl, ghost), to_right)
        left = send(src, block(1, dzl, ghost), to_left)
        return {2: far, 3: right, 1: left}

    def along_z(dt, ghost):
        return send(block(dt, 0, ghost), block(dt, 1, ghost), to_z)

    cores = []

    def to_other(dt, dzl, ghost):
        cores.append(send(block(dt, dzl, ghost), gathered.at[1, dt, dzl, ghost], to_core))

    gz0 = along_z(0, 1)
    ox = along_x(0, 0)
    oz0 = along_z(0, 0)
    gx = along_x(0, 1)
    cores.append(send(gathered.at[0, 0, 0], gathered.at[1, 0, 0], to_core))
    gz0.wait_recv()
    gzx = along_x(1, 1)
    to_other(0, 1, 1)
    ozs = {}
    for dt in (3, 1, 2):
        ox[dt].wait_recv()
        ozs[dt] = along_z(dt, 0)
        to_other(dt, 0, 0)
    oz0.wait_recv()
    to_other(0, 1, 0)
    for dt in (3, 1, 2):
        gx[dt].wait_recv()
        to_other(dt, 0, 1)
    for dt in (3, 1, 2):
        ozs[dt].wait_recv()
        to_other(dt, 1, 0)
        gzx[dt].wait_recv()
        to_other(dt, 1, 1)
    for copy in cores:
        copy.wait_recv()

    for first, width, residue in GROUPS:
        at = pl.ds(first, width)
        highs, lows = [], []
        for dc in range(2):
            for dt in range(4):
                lines = gathered[dc, dt, :, :, :, at].reshape(32, width)
                high, low = split(lines * response[dt : dt + 1, at])
                highs.append(high)
                lows.append(low)
        back = back_rows[...]
        u = dot(back, jnp.concatenate(highs, 0)) + dot(back, jnp.concatenate(lows, 0))
        high, low = split(u)
        if width == 512:
            th, tl = inv_big[0, residue - 1], inv_big[1, residue - 1]
        else:
            th, tl = inv_small[0, residue // 4], inv_small[1, residue // 4]
        spectral[:, at] = dot(high, th) + dot(low, th) + dot(high, tl)

    def part(first):
        return spectral[:, first : first + PART]

    g0, g4 = part(0), part(256)
    r1, i1, r2, i2, r3, i3 = (part(512 + PART * i) for i in range(6))
    p, q = g0 + g4, g0 - g4
    pr, ps = p + r2, p - r2
    qm, qp = q - i2, q + i2
    r13, i31 = r1 + r3, i3 - i1
    rd, im = r1 - r3, i1 + i3
    v, w = root * (rd - im), root * (rd + im)
    ys = (pr + r13, qm + v, ps + i31, qp - w, pr - r13, qm - v, ps - i31, qp + w)
    for a in range(8):
        at = pl.ds(PART * a, PART)
        out[:, :, at] = vol[:, :, at] + ys[a].reshape(LAYERS, ROWS, PART)

    for copy in sent:
        copy.wait_send()
    for copy, there in halos:
        pl.when(there)(copy.wait_send)


def body(tiles, tables, volume, measured, ray_offset, defocus):
    fwd_big, fwd_small, inv_big, inv_small, line = tables
    hbm = pl.BlockSpec(memory_space=pltpu.HBM)

    def f(*shape):
        return pltpu.VMEM(shape, f32)

    return pl.pallas_call(
        functools.partial(kernel, tiles),
        out_shape=jax.ShapeDtypeStruct(volume.shape, f32),
        in_specs=[hbm] * 9,
        out_specs=pl.BlockSpec(memory_space=pltpu.VMEM),
        scratch_shapes=[
            pltpu.SMEM(ray_offset.shape, jnp.int32),
            pltpu.SMEM(defocus.shape, jnp.int32),
            f(*volume.shape),
            f(*line.shape),
            f(TILTS, LINE),
            pltpu.VMEM((128, 256), bf16),
            pltpu.VMEM(fwd_big.shape, bf16),
            pltpu.VMEM(fwd_small.shape, bf16),
            pltpu.VMEM(inv_big.shape, bf16),
            pltpu.VMEM(inv_small.shape, bf16),
            f(2, 8, LINE),
            pltpu.VMEM((256, LINE), bf16),
            f(4, 2, 8, LINE),
            f(2, 4, 8, LINE),
            f(4, 2, 8, LINE),
            f(2, 4, 8, LINE),
            f(4, 2, 8, LINE),
            f(2, 4, 8, LINE),
            f(3, 2, 8, LINE),
            f(8, LINE),
            f(4, 8, LINE),
            f(3, 8, LINE),
            f(8, LINE),
            f(8, LINE),
            f(2, 4, 2, 2, 8, LINE),
            f(128, LINE),
            pltpu.SemaphoreType.DMA((9,)),
            pltpu.SemaphoreType.DMA((64,)),
            pltpu.SemaphoreType.DMA((64,)),
        ],
        compiler_params=pltpu.CompilerParams(
            collective_id=0, has_side_effects=True, vmem_limit_bytes=60 * 1024 * 1024
        ),
        name="step",
    )(ray_offset, defocus, volume, measured, line, fwd_big, fwd_small, inv_big, inv_small)


def solution(mesh):
    placed = (P("gz", "xy", None), P(None, "xy", None), P(), P())
    tables = tuple(dft_tables())
    return jax.shard_map(
        functools.partial(body, mesh.shape["xy"], tables),
        mesh=mesh,
        in_specs=placed,
        out_specs=P("gz", "xy", None),
        check_vma=False,
    )
```

```python
import functools
import math

import jax
import jax.numpy as jnp
import ml_dtypes
import numpy as np
from jax import lax
from jax.experimental import pallas as pl
from jax.experimental.pallas import tpu as pltpu
from jax.sharding import PartitionSpec as P

HALO = 16
LINE = 2048
PART = 256
ROWS = 32
LAYERS = 4
TILTS = 4
SUM_PARTS = 2
SEMAPHORES = 64
GATHER_PARTS = 1

pixel_size = 4.0
wavelength = 0.0197
contrast = 0.07
amplitude_root = math.sqrt(1.0 - 0.07 * 0.07)
f32 = jnp.float32
bf16 = jnp.bfloat16
MESH = pl.DeviceIdType.MESH

GROUPS = ((0, 256, 0), (256, 256, 4), (512, 512, 1), (1024, 512, 2), (1536, 512, 3))


def halves(table):
    high = table.astype(ml_dtypes.bfloat16)
    low = (table - high.astype(np.float64)).astype(ml_dtypes.bfloat16)
    return np.stack([high, low])


def dft_tables():
    b = np.arange(PART, dtype=np.int64)[:, None]
    tables, freq, scale = {}, [], []
    for _, width, residue in GROUPS:
        if residue == 0:
            re, im = np.arange(0, 129), np.arange(1, 128)
        elif residue == 4:
            re = im = np.arange(0, 128)
        else:
            re = im = np.arange(0, 256)
        f_re, f_im = residue + 8 * re, residue + 8 * im
        turn_re = 2 * np.pi / LINE * (b * f_re % LINE)
        turn_im = 2 * np.pi / LINE * (b * f_im % LINE)
        real_in = np.concatenate([np.cos(turn_re), -np.sin(turn_im)], 1)
        if width == 512:
            imag_in = np.concatenate([np.sin(turn_re), np.cos(turn_im)], 1)
            real_in = np.concatenate([real_in, imag_in], 0)
        tables[residue] = real_in
        f = np.concatenate([f_re, f_im])
        folded = np.where(2 * f < LINE, f, f - LINE)
        freq.append(folded / (LINE * pixel_size))
        scale.append(np.where((f == 0) | (f == LINE // 2), 1.0, 2.0) / (LINE * TILTS))
    big = np.stack([tables[1], tables[2], tables[3]])
    small = np.stack([tables[0], tables[4]])
    line = np.stack([np.concatenate(freq), np.concatenate(scale)]).astype(np.float32)
    return (
        halves(big),
        halves(small),
        halves(big.transpose(0, 2, 1)),
        halves(small.transpose(0, 2, 1)),
        line,
    )


def split(x):
    high = x.astype(bf16)
    low = (x - high.astype(f32)).astype(bf16)
    return high, low


def dot(a, b):
    return jnp.dot(a, b, preferred_element_type=f32)


def kernel(
    tiles,
    ray_hbm,
    defocus_hbm,
    vol_hbm,
    meas,
    line_hbm,
    fwd_big_hbm,
    fwd_small_hbm,
    inv_big_hbm,
    inv_small_hbm,
    out,
    ray,
    defocus,
    vol,
    line,
    response,
    back_rows,
    fwd_big,
    fwd_small,
    inv_big,
    inv_small,
    meas_rows,
    vcat,
    other_g,
    other_o,
    mine_g,
    mine_o,
    core_g,
    core_o,
    fin_g,
    zin_g,
    zin_o,
    fin_o,
    halo_g,
    halo_o,
    gathered,
    spectral,
    terms,
    local_sem,
    ss,
    rs,
):
    gz = lax.axis_index("gz")
    xy = lax.axis_index("xy")
    X = gz // 4
    zl = (gz // 2) % 2
    c = gz % 2
    to_core = {"gz": gz + 1 - 2 * c}
    to_z = {"gz": gz + 2 - 4 * zl}
    to_right = {"gz": (gz + 4) % 16}
    to_left = {"gz": (gz + 12) % 16}
    to_far = {"gz": (gz + 8) % 16}
    step = 1 - 2 * zl
    has_ahead = (xy + step >= 0) & (xy + step < tiles)
    has_behind = (xy - step >= 0) & (xy - step < tiles)
    to_ahead = {"xy": (xy + step + tiles) % tiles}
    to_behind = {"xy": (xy - step + tiles) % tiles}
    partners = (to_core, to_z, to_right, to_left, to_far)
    barrier = pltpu.get_barrier_semaphore()

    def greet(partner):
        pl.semaphore_signal(barrier, inc=1, device_id=partner, device_id_type=MESH)

    for partner in partners:
        greet(partner)
    pl.when(has_ahead)(lambda: greet(to_ahead))
    pl.when(has_behind)(lambda: greet(to_behind))
    greetings = len(partners) + has_ahead.astype(jnp.int32) + has_behind.astype(jnp.int32)

    k_own = zl * 2 + c
    meas_hbm = meas.at[X, pl.ds(pl.multiple_of(8 * k_own, 8), 8)]
    quarter = [pl.ds(512 * j, 512) for j in range(4)]
    start_copies = [pltpu.make_async_copy(ray_hbm, ray, local_sem.at[5])] + [
        pltpu.make_async_copy(vol_hbm.at[:, :, quarter[j]], vol.at[:, :, quarter[j]], local_sem.at[8 + j])
        for j in range(4)
    ]
    for copy in start_copies:
        copy.start()

    @pl.when(jnp.logical_not(has_behind))
    def _():
        halo_g[...] = jnp.zeros_like(halo_g)

    @pl.when(jnp.logical_not(has_ahead))
    def _():
        halo_o[...] = jnp.zeros_like(halo_o)
        meas_rows[1] = jnp.zeros((8, LINE), f32)

    locals_ = [
        pltpu.make_async_copy(defocus_hbm, defocus, local_sem.at[7]),
        pltpu.make_async_copy(line_hbm, line, local_sem.at[6]),
        pltpu.make_async_copy(meas_hbm, meas_rows.at[0], local_sem.at[0]),
        pltpu.make_async_copy(fwd_big_hbm, fwd_big, local_sem.at[1]),
        pltpu.make_async_copy(fwd_small_hbm, fwd_small, local_sem.at[2]),
        pltpu.make_async_copy(inv_big_hbm, inv_big, local_sem.at[3]),
        pltpu.make_async_copy(inv_small_hbm, inv_small, local_sem.at[4]),
    ]
    count = [0]
    sent = []
    halos = []

    def send(src, dst, where):
        i = count[0]
        count[0] += 1
        copy = pltpu.make_async_remote_copy(
            src_ref=src, dst_ref=dst, send_sem=ss.at[i], recv_sem=rs.at[i],
            device_id=where, device_id_type=MESH,
        )
        copy.start()
        sent.append(copy)
        return copy

    start_copies[0].wait()
    def send_halo(src, dst, where, there, back):
        i = count[0]
        count[0] += 1
        copy = pltpu.make_async_remote_copy(
            src_ref=src, dst_ref=dst, send_sem=ss.at[i], recv_sem=rs.at[i],
            device_id=where, device_id_type=MESH,
        )
        pl.when(there)(copy.start)
        halos.append((copy, there))
        return lambda: pl.when(back)(copy.wait_recv)

    shift, far = {}, {}
    for dt in range(4):
        t = (X + dt) % 4
        for z in range(LAYERS):
            offset = ray[t, gz * LAYERS + z]
            shift[dt, z] = offset >> 3
            far[dt, z] = (offset & 7).astype(f32) * 0.125

    col = lax.broadcasted_iota(jnp.int32, (8, 128), 1)
    sub = lax.broadcasted_iota(jnp.int32, (8, 128), 0)
    layer = col // ROWS
    target, near_row, far_row = {}, {}, {}
    for dt in range(4):
        s = jnp.zeros((8, 128), jnp.int32)
        w = jnp.zeros((8, 128), f32)
        for z in range(LAYERS):
            s = jnp.where(layer == z, shift[dt, z], s)
            w = jnp.where(layer == z, far[dt, z], w)
        target[dt] = col % ROWS - s
        near_row[dt], far_row[dt] = 1.0 - w, w

    def first_ext(zone, core, ghost):
        base = 8 * (zone * 2 + core)
        if ghost:
            base = base + 32 - 64 * zone
        return base

    def weights(core, ghost, dt, dzl):
        zone = zl ^ dzl
        e = sub + first_ext(zone, core, ghost)
        return jnp.where(e == target[dt], near_row[dt], 0.0) + jnp.where(
            e == target[dt] - 1, far_row[dt], 0.0
        )

    def lhs(core):
        blocks = [weights(core, True, dt, dzl) for dt in range(4) for dzl in range(2)]
        blocks += [weights(core, False, dt, dzl) for dzl in range(2) for dt in range(4)]
        w = jnp.concatenate(blocks, 0).astype(bf16)
        return jnp.concatenate([w, w], 1)

    def project(core, to_g, to_o, fill=False):
        w = lhs(core)
        for j, at in enumerate(quarter):
            if fill:
                start_copies[1 + j].wait()
                high, low = split(vol[:, :, at].reshape(LAYERS * ROWS, 512))
                vcat[0:128, at] = high
                vcat[128:256, at] = low
            p = dot(w, vcat[:, at])
            to_g[:, :, :, at] = p[0:64].reshape(4, 2, 8, 512)
            to_o[:, :, :, at] = p[64:128].reshape(2, 4, 8, 512)

    project(1 - c, other_g, other_o, fill=True)
    pl.semaphore_wait(barrier, greetings)
    cg, co = {}, {}
    cg[2] = send(other_g.at[2], core_g.at[2], to_core)
    co[1] = send(other_o.at[1], core_o.at[1], to_core)
    cg[1] = send(other_g.at[1], core_g.at[1], to_core)
    cg[3] = send(other_g.at[3], core_g.at[3], to_core)
    co[0] = send(other_o.at[0], core_o.at[0], to_core)
    cg[0] = send(other_g.at[0], core_g.at[0], to_core)
    for copy in locals_:
        copy.start()
    meas_wait = send_halo(meas_hbm, meas_rows.at[1], to_behind, has_behind, has_ahead)
    project(c, mine_g, mine_o)

    def add(dst, src):
        dst[...] = dst[...] + src[...]

    width = LINE // SUM_PARTS
    parts = [pl.ds(width * i, width) for i in range(SUM_PARTS)]
    cg[2].wait_recv()
    add(mine_g.at[2], core_g.at[2])
    gx, ox, oz = {}, {}, {}
    for i, at in enumerate(parts):
        gx[2, i] = send(mine_g.at[2, :, :, at], fin_g.at[2, :, :, at], to_far)
    co[1].wait_recv()
    add(mine_o.at[1], core_o.at[1])
    for i, at in enumerate(parts):
        for dt in (2, 1, 3, 0):
            oz[dt, i] = send(mine_o.at[1, dt, :, at], zin_o.at[dt, :, at], to_z)
    cg[1].wait_recv()
    add(mine_g.at[1], core_g.at[1])
    cg[3].wait_recv()
    add(mine_g.at[3], core_g.at[3])
    for i, at in enumerate(parts):
        gx[1, i] = send(mine_g.at[1, :, :, at], fin_g.at[0, :, :, at], to_right)
        gx[3, i] = send(mine_g.at[3, :, :, at], fin_g.at[1, :, :, at], to_left)
    co[0].wait_recv()
    add(mine_o.at[0], core_o.at[0])
    cg[0].wait_recv()
    add(mine_g.at[0], core_g.at[0])

    for copy in locals_[:2]:
        copy.wait()
    tilt_row = lax.broadcasted_iota(jnp.int32, (TILTS, 1), 0)
    number = jnp.zeros((TILTS, 1), f32)
    for dt in range(4):
        number = jnp.where(tilt_row == dt, defocus[(X + dt) % 4, gz].astype(f32), number)
    frequency = line[0:1, :]
    phase = math.pi * wavelength * number * frequency * frequency
    response[...] = (
        -(amplitude_root * jnp.sin(phase) + contrast * jnp.cos(phase)) * line[1:2, :]
    )

    gcol = lax.broadcasted_iota(jnp.int32, (ROWS, 256), 1)
    grow = lax.broadcasted_iota(jnp.int32, (ROWS, 256), 0)
    zone = zl ^ ((gcol >> 4) & 1)
    place = 8 * (zone * 2 + (c ^ (gcol >> 7))) + (gcol & 7)
    place = place + ((gcol >> 3) & 1) * (32 - 64 * zone)
    tilt = (gcol >> 5) & 3
    there = place + xy * ROWS
    legal = (there >= 0) & (there < tiles * ROWS)
    back = []
    for z in range(LAYERS):
        s = jnp.zeros((ROWS, 256), jnp.int32)
        w = jnp.zeros((ROWS, 256), f32)
        for dt in range(4):
            s = jnp.where(tilt == dt, shift[dt, z], s)
            w = jnp.where(tilt == dt, far[dt, z], w)
        delta = place + s - grow
        both = jnp.where(delta == 0, 1.0 - w, 0.0) + jnp.where(delta == -1, w, 0.0)
        back.append(jnp.where(legal, both, 0.0))
    back_rows[...] = jnp.concatenate(back, 0).astype(bf16)

    gz_, waits = {}, []
    for i, at in enumerate(parts):
        for dt, slot, where in ((2, 2, to_far), (1, 0, to_right), (3, 1, to_left)):
            oz[dt, i].wait_recv()
            add(mine_o.at[0, dt, :, at], zin_o.at[dt, :, at])
            ox[dt, i] = send(mine_o.at[0, dt, :, at], fin_o.at[slot, :, at], where)
    for i, at in enumerate(parts):
        for dt in (2, 1, 3):
            gx[dt, i].wait_recv()
        mine_g[0, :, :, at] = (mine_g[0, :, :, at] + fin_g[0, :, :, at]) + (
            fin_g[1, :, :, at] + fin_g[2, :, :, at]
        )
        gz_[i] = send(mine_g.at[0, 1, :, at], zin_g.at[:, at], to_z)
    for i, at in enumerate(parts):
        oz[0, i].wait_recv()
        for dt in (2, 1, 3):
            ox[dt, i].wait_recv()
        mine_o[0, 0, :, at] = (
            (mine_o[0, 0, :, at] + zin_o[0, :, at])
            + (fin_o[0, :, at] + fin_o[1, :, at])
            + fin_o[2, :, at]
        )
        waits.append(
            send_halo(mine_o.at[0, 0, :, at], halo_o.at[:, at], to_behind, has_behind, has_ahead)
        )
        gz_[i].wait_recv()
        add(mine_g.at[0, 0, :, at], zin_g.at[:, at])
        waits.append(
            send_halo(mine_g.at[0, 0, :, at], halo_g.at[:, at], to_ahead, has_ahead, has_behind)
        )
    for copy in locals_[2:]:
        copy.wait()

    meas_wait()
    for wait in waits:
        wait()
    ray_norm = float(TILTS * 16) ** (-0.5)
    own_sum = mine_o[0, 0] + jnp.where(has_behind, halo_g[...], 0.0)
    own_rows = meas_rows[0] - ray_norm * own_sum
    ghost_rows = meas_rows[1] - ray_norm * (mine_g[0, 0] + halo_o[...])
    ghost_rows = jnp.where(has_ahead, ghost_rows, 0.0)
    residual = jnp.concatenate([own_rows, ghost_rows], 0)

    x = [residual[:, PART * a : PART * (a + 1)] for a in range(8)]
    root = math.sqrt(0.5)
    s04, d04 = x[0] + x[4], x[0] - x[4]
    s26, d26 = x[2] + x[6], x[2] - x[6]
    s15, d15 = x[1] + x[5], x[1] - x[5]
    s37, d37 = x[3] + x[7], x[3] - x[7]
    even, odd = s04 + s26, s15 + s37
    m = root * (d15 - d37)
    n = root * (d15 + d37)
    inputs = {
        0: even + odd,
        4: even - odd,
        1: jnp.concatenate([d04 + m, -(d26 + n)], 1),
        2: jnp.concatenate([s04 - s26, s37 - s15], 1),
        3: jnp.concatenate([d04 - m, d26 - n], 1),
    }
    for first, width, residue in GROUPS:
        high, low = split(inputs[residue])
        if width == 512:
            th, tl = fwd_big[0, residue - 1], fwd_big[1, residue - 1]
        else:
            th, tl = fwd_small[0, residue // 4], fwd_small[1, residue // 4]
        both = dot(jnp.concatenate([high, low], 0), th)
        lines = both[0:16] + both[16:32] + dot(high, tl)
        gathered[0, 0, 0, :, :, first : first + width] = lines.reshape(2, 8, width)

    piece = LINE // GATHER_PARTS
    pieces = [pl.ds(piece * i, piece) for i in range(GATHER_PARTS)]

    def block(dt, dzl, ghost, i):
        return gathered.at[0, dt, dzl, ghost, :, pieces[i]]

    def along_x(dzl, ghost, i):
        src = block(0, dzl, ghost, i)
        return {
            2: send(src, block(2, dzl, ghost, i), to_far),
            3: send(src, block(3, dzl, ghost, i), to_right),
            1: send(src, block(1, dzl, ghost, i), to_left),
        }

    def along_z(dt, ghost, i):
        return send(block(dt, 0, ghost, i), block(dt, 1, ghost, i), to_z)

    passed = {}

    def to_other(dt, dzl, ghost, i):
        src = block(dt, dzl, ghost, i)
        passed.setdefault((dt, dzl), []).append(
            send(src, gathered.at[1, dt, dzl, ghost, :, pieces[i]], to_core)
        )

    def scale(core, dt, dzl):
        lines = gathered[core, dt, dzl].reshape(16, LINE) * response[dt : dt + 1, :]
        high, low = split(lines)
        first = 256 * core + 32 * dt + 16 * dzl
        terms[first : first + 16, :] = high
        terms[first + 128 : first + 144, :] = low

    def combine(core):
        w = back_rows[:, 128 * core : 128 * core + 128]
        w = jnp.concatenate([w, w], 1)
        for at in quarter:
            u = dot(w, terms[256 * core : 256 * core + 256, at])
            spectral[:, at] = spectral[:, at] + u if core else u

    n = range(GATHER_PARTS)
    az, bx, bz, cx, cz = {}, {}, {}, {}, {}
    for i in n:
        az[i] = along_z(0, 1, i)
        bx[i] = along_x(0, 0, i)
        bz[0, i] = along_z(0, 0, i)
    for i in n:
        cx[i] = along_x(0, 1, i)
    for i in n:
        to_other(0, 0, 0, i)
        to_other(0, 0, 1, i)
    for i in n:
        az[i].wait_recv()
        cz[i] = along_x(1, 1, i)
        to_other(0, 1, 1, i)
    for i in n:
        for dt in (3, 1, 2):
            bx[i][dt].wait_recv()
            bz[dt, i] = along_z(dt, 0, i)
            to_other(dt, 0, 0, i)
    scale(0, 0, 0)
    for i in n:
        bz[0, i].wait_recv()
        to_other(0, 1, 0, i)
    scale(0, 0, 1)
    for dt in (3, 1, 2):
        for i in n:
            cx[i][dt].wait_recv()
            to_other(dt, 0, 1, i)
        scale(0, dt, 0)
    for copy in passed[0, 0]:
        copy.wait_recv()
    scale(1, 0, 0)
    for dt in (3, 1, 2):
        for i in n:
            bz[dt, i].wait_recv()
            to_other(dt, 1, 0, i)
            cz[i][dt].wait_recv()
            to_other(dt, 1, 1, i)
        scale(0, dt, 1)
    combine(0)
    for key in ((0, 1), (3, 0), (1, 0), (2, 0), (3, 1), (1, 1), (2, 1)):
        for copy in passed[key]:
            copy.wait_recv()
        scale(1, *key)
    combine(1)

    for first, width, residue in GROUPS:
        at = pl.ds(first, width)
        high, low = split(spectral[:, at])
        if width == 512:
            th, tl = inv_big[0, residue - 1], inv_big[1, residue - 1]
        else:
            th, tl = inv_small[0, residue // 4], inv_small[1, residue // 4]
        spectral[:, at] = dot(high, th) + dot(low, th) + dot(high, tl)

    def part(first):
        return spectral[:, first : first + PART]

    g0, g4 = part(0), part(256)
    r1, i1, r2, i2, r3, i3 = (part(512 + PART * i) for i in range(6))
    p, q = g0 + g4, g0 - g4
    pr, ps = p + r2, p - r2
    qm, qp = q - i2, q + i2
    r13, i31 = r1 + r3, i3 - i1
    rd, im = r1 - r3, i1 + i3
    v, w = root * (rd - im), root * (rd + im)
    ys = (pr + r13, qm + v, ps + i31, qp - w, pr - r13, qm - v, ps - i31, qp + w)
    for a in range(8):
        at = pl.ds(PART * a, PART)
        out[:, :, at] = vol[:, :, at] + ys[a].reshape(LAYERS, ROWS, PART)

    for copy in sent:
        copy.wait_send()
    for copy, there in halos:
        pl.when(there)(copy.wait_send)


def body(tiles, tables, volume, measured, ray_offset, defocus):
    fwd_big, fwd_small, inv_big, inv_small, line = tables
    hbm = pl.BlockSpec(memory_space=pltpu.HBM)

    def f(*shape):
        return pltpu.VMEM(shape, f32)

    arrays = (ray_offset, defocus, volume, measured, line, fwd_big, fwd_small, inv_big, inv_small)
    return pl.pallas_call(
        functools.partial(kernel, tiles),
        out_shape=pltpu.VMEM(volume.shape, f32),
        in_specs=[hbm] * 9,
        out_specs=pl.BlockSpec(memory_space=pltpu.VMEM),
        scratch_shapes=[
            pltpu.SMEM(ray_offset.shape, jnp.int32),
            pltpu.SMEM(defocus.shape, jnp.int32),
            f(*volume.shape),
            f(*line.shape),
            f(TILTS, LINE),
            pltpu.VMEM((128, 256), bf16),
            pltpu.VMEM(fwd_big.shape, bf16),
            pltpu.VMEM(fwd_small.shape, bf16),
            pltpu.VMEM(inv_big.shape, bf16),
            pltpu.VMEM(inv_small.shape, bf16),
            f(2, 8, LINE),
            pltpu.VMEM((256, LINE), bf16),
            f(4, 2, 8, LINE),
            f(2, 4, 8, LINE),
            f(4, 2, 8, LINE),
            f(2, 4, 8, LINE),
            f(4, 2, 8, LINE),
            f(2, 4, 8, LINE),
            f(3, 2, 8, LINE),
            f(8, LINE),
            f(4, 8, LINE),
            f(3, 8, LINE),
            f(8, LINE),
            f(8, LINE),
            f(2, 4, 2, 2, 8, LINE),
            f(128, LINE),
            pltpu.VMEM((512, LINE), bf16),
            pltpu.SemaphoreType.DMA((12,)),
            pltpu.SemaphoreType.DMA((SEMAPHORES,)),
            pltpu.SemaphoreType.DMA((SEMAPHORES,)),
        ],
        compiler_params=pltpu.CompilerParams(
            collective_id=0, has_side_effects=True, vmem_limit_bytes=40 * 1024 * 1024
        ),
        name="step",
    )(*(pltpu.with_memory_space_constraint(a, pltpu.HBM) for a in arrays))


def solution(mesh):
    placed = (P("gz", "xy", None), P(None, "xy", None), P(), P())
    tables = tuple(dft_tables())
    return jax.shard_map(
        functools.partial(body, mesh.shape["xy"], tables),
        mesh=mesh,
        in_specs=placed,
        out_specs=P("gz", "xy", None),
        check_vma=False,
    )
```

```python
import functools
import math

import jax
import jax.numpy as jnp
import ml_dtypes
import numpy as np
from jax import lax
from jax.experimental import pallas as pl
from jax.experimental.pallas import tpu as pltpu
from jax.sharding import PartitionSpec as P

HALO = 16
LINE = 2048
PART = 256
ROWS = 32
LAYERS = 4
TILTS = 4
SUM_PARTS = 2
SEMAPHORES = 64

pixel_size = 4.0
wavelength = 0.0197
contrast = 0.07
amplitude_root = math.sqrt(1.0 - 0.07 * 0.07)
f32 = jnp.float32
bf16 = jnp.bfloat16
MESH = pl.DeviceIdType.MESH

GROUPS = ((0, 256, 0), (256, 256, 4), (512, 512, 1), (1024, 512, 2), (1536, 512, 3))


def halves(table):
    high = table.astype(ml_dtypes.bfloat16)
    low = (table - high.astype(np.float64)).astype(ml_dtypes.bfloat16)
    return np.stack([high, low])


def dft_tables():
    b = np.arange(PART, dtype=np.int64)[:, None]
    tables, freq, scale = {}, [], []
    for _, width, residue in GROUPS:
        if residue == 0:
            re, im = np.arange(0, 129), np.arange(1, 128)
        elif residue == 4:
            re = im = np.arange(0, 128)
        else:
            re = im = np.arange(0, 256)
        f_re, f_im = residue + 8 * re, residue + 8 * im
        turn_re = 2 * np.pi / LINE * (b * f_re % LINE)
        turn_im = 2 * np.pi / LINE * (b * f_im % LINE)
        real_in = np.concatenate([np.cos(turn_re), -np.sin(turn_im)], 1)
        if width == 512:
            imag_in = np.concatenate([np.sin(turn_re), np.cos(turn_im)], 1)
            real_in = np.concatenate([real_in, imag_in], 0)
        tables[residue] = real_in
        f = np.concatenate([f_re, f_im])
        folded = np.where(2 * f < LINE, f, f - LINE)
        freq.append(folded / (LINE * pixel_size))
        scale.append(np.where((f == 0) | (f == LINE // 2), 1.0, 2.0) / (LINE * TILTS))
    big = np.stack([tables[1], tables[2], tables[3]])
    small = np.stack([tables[0], tables[4]])
    line = np.stack([np.concatenate(freq), np.concatenate(scale)]).astype(np.float32)
    return (
        halves(big),
        halves(small),
        halves(big.transpose(0, 2, 1)),
        halves(small.transpose(0, 2, 1)),
        line,
    )


def split(x):
    high = x.astype(bf16)
    low = (x - high.astype(f32)).astype(bf16)
    return high, low


def dot(a, b):
    return jnp.dot(a, b, preferred_element_type=f32)


def kernel(
    tiles,
    ray_hbm,
    defocus_hbm,
    vol_hbm,
    meas,
    line_hbm,
    fwd_big_hbm,
    fwd_small_hbm,
    inv_big_hbm,
    inv_small_hbm,
    out,
    ray,
    defocus,
    vol,
    line,
    response,
    back_rows,
    fwd_big,
    fwd_small,
    inv_big,
    inv_small,
    meas_rows,
    vcat,
    other_g,
    other_o,
    mine_g,
    mine_o,
    core_g,
    core_o,
    fin_g,
    zin_g,
    zin_o,
    fin_o,
    halo_g,
    halo_o,
    gathered,
    spectral,
    terms,
    local_sem,
    ss,
    rs,
):
    gz = lax.axis_index("gz")
    xy = lax.axis_index("xy")
    X = gz // 4
    zl = (gz // 2) % 2
    c = gz % 2
    to_core = {"gz": gz + 1 - 2 * c}
    to_z = {"gz": gz + 2 - 4 * zl}
    to_right = {"gz": (gz + 4) % 16}
    to_left = {"gz": (gz + 12) % 16}
    to_far = {"gz": (gz + 8) % 16}
    step = 1 - 2 * zl
    has_ahead = (xy + step >= 0) & (xy + step < tiles)
    has_behind = (xy - step >= 0) & (xy - step < tiles)
    to_ahead = {"xy": (xy + step + tiles) % tiles}
    to_behind = {"xy": (xy - step + tiles) % tiles}
    partners = (to_core, to_z, to_right, to_left, to_far)
    barrier = pltpu.get_barrier_semaphore()

    def greet(partner):
        pl.semaphore_signal(barrier, inc=1, device_id=partner, device_id_type=MESH)

    for partner in partners:
        greet(partner)
    pl.when(has_ahead)(lambda: greet(to_ahead))
    pl.when(has_behind)(lambda: greet(to_behind))
    greetings = len(partners) + has_ahead.astype(jnp.int32) + has_behind.astype(jnp.int32)

    k_own = zl * 2 + c
    meas_hbm = meas.at[X, pl.ds(pl.multiple_of(8 * k_own, 8), 8)]
    quarter = [pl.ds(512 * j, 512) for j in range(4)]
    start_copies = [pltpu.make_async_copy(ray_hbm, ray, local_sem.at[5])] + [
        pltpu.make_async_copy(vol_hbm.at[:, :, quarter[j]], vol.at[:, :, quarter[j]], local_sem.at[8 + j])
        for j in range(4)
    ]
    for copy in start_copies:
        copy.start()

    @pl.when(jnp.logical_not(has_behind))
    def _():
        halo_g[...] = jnp.zeros_like(halo_g)

    @pl.when(jnp.logical_not(has_ahead))
    def _():
        halo_o[...] = jnp.zeros_like(halo_o)
        meas_rows[1] = jnp.zeros((8, LINE), f32)

    locals_ = [
        pltpu.make_async_copy(defocus_hbm, defocus, local_sem.at[7]),
        pltpu.make_async_copy(line_hbm, line, local_sem.at[6]),
        pltpu.make_async_copy(meas_hbm, meas_rows.at[0], local_sem.at[0]),
        pltpu.make_async_copy(fwd_big_hbm, fwd_big, local_sem.at[1]),
        pltpu.make_async_copy(fwd_small_hbm, fwd_small, local_sem.at[2]),
        pltpu.make_async_copy(inv_big_hbm, inv_big, local_sem.at[3]),
        pltpu.make_async_copy(inv_small_hbm, inv_small, local_sem.at[4]),
    ]
    count = [0]
    sent = []
    halos = []

    def send(src, dst, where):
        i = count[0]
        count[0] += 1
        copy = pltpu.make_async_remote_copy(
            src_ref=src, dst_ref=dst, send_sem=ss.at[i], recv_sem=rs.at[i],
            device_id=where, device_id_type=MESH,
        )
        copy.start()
        sent.append(copy)
        return copy

    start_copies[0].wait()
    def send_halo(src, dst, where, there, back):
        i = count[0]
        count[0] += 1
        copy = pltpu.make_async_remote_copy(
            src_ref=src, dst_ref=dst, send_sem=ss.at[i], recv_sem=rs.at[i],
            device_id=where, device_id_type=MESH,
        )
        pl.when(there)(copy.start)
        halos.append((copy, there))
        return lambda: pl.when(back)(copy.wait_recv)

    shift, far = {}, {}
    for dt in range(4):
        t = (X + dt) % 4
        for z in range(LAYERS):
            offset = ray[t, gz * LAYERS + z]
            shift[dt, z] = offset >> 3
            far[dt, z] = (offset & 7).astype(f32) * 0.125

    col = lax.broadcasted_iota(jnp.int32, (8, 128), 1)
    sub = lax.broadcasted_iota(jnp.int32, (8, 128), 0)
    layer = col // ROWS
    target, near_row, far_row = {}, {}, {}
    for dt in range(4):
        s = jnp.zeros((8, 128), jnp.int32)
        w = jnp.zeros((8, 128), f32)
        for z in range(LAYERS):
            s = jnp.where(layer == z, shift[dt, z], s)
            w = jnp.where(layer == z, far[dt, z], w)
        target[dt] = col % ROWS - s
        near_row[dt], far_row[dt] = 1.0 - w, w

    def first_ext(zone, core, ghost):
        base = 8 * (zone * 2 + core)
        if ghost:
            base = base + 32 - 64 * zone
        return base

    def weights(core, ghost, dt, dzl):
        zone = zl ^ dzl
        e = sub + first_ext(zone, core, ghost)
        return jnp.where(e == target[dt], near_row[dt], 0.0) + jnp.where(
            e == target[dt] - 1, far_row[dt], 0.0
        )

    def lhs(core):
        blocks = [weights(core, True, dt, dzl) for dt in range(4) for dzl in range(2)]
        blocks += [weights(core, False, dt, dzl) for dzl in range(2) for dt in range(4)]
        w = jnp.concatenate(blocks, 0).astype(bf16)
        return jnp.concatenate([w, w], 1)

    def project(core, to_g, to_o, fill=False):
        w = lhs(core)
        for j, at in enumerate(quarter):
            if fill:
                start_copies[1 + j].wait()
                high, low = split(vol[:, :, at].reshape(LAYERS * ROWS, 512))
                vcat[0:128, at] = high
                vcat[128:256, at] = low
            p = dot(w, vcat[:, at])
            to_g[:, :, :, at] = p[0:64].reshape(4, 2, 8, 512)
            to_o[:, :, :, at] = p[64:128].reshape(2, 4, 8, 512)

    project(1 - c, other_g, other_o, fill=True)
    pl.semaphore_wait(barrier, greetings)
    cg, co = {}, {}
    cg[2] = send(other_g.at[2], core_g.at[2], to_core)
    co[1] = send(other_o.at[1], core_o.at[1], to_core)
    cg[1] = send(other_g.at[1], core_g.at[1], to_core)
    cg[3] = send(other_g.at[3], core_g.at[3], to_core)
    co[0] = send(other_o.at[0], core_o.at[0], to_core)
    cg[0] = send(other_g.at[0], core_g.at[0], to_core)
    for copy in locals_:
        copy.start()
    meas_wait = send_halo(meas_hbm, meas_rows.at[1], to_behind, has_behind, has_ahead)
    project(c, mine_g, mine_o)

    def add(dst, src):
        dst[...] = dst[...] + src[...]

    width = LINE // SUM_PARTS
    parts = [pl.ds(width * i, width) for i in range(SUM_PARTS)]
    cg[2].wait_recv()
    add(mine_g.at[2], core_g.at[2])
    gx, ox, oz = {}, {}, {}
    for i, at in enumerate(parts):
        gx[2, i] = send(mine_g.at[2, :, :, at], fin_g.at[2, :, :, at], to_far)
    co[1].wait_recv()
    add(mine_o.at[1], core_o.at[1])
    for i, at in enumerate(parts):
        for dt in (2, 1, 3, 0):
            oz[dt, i] = send(mine_o.at[1, dt, :, at], zin_o.at[dt, :, at], to_z)
    cg[1].wait_recv()
    add(mine_g.at[1], core_g.at[1])
    cg[3].wait_recv()
    add(mine_g.at[3], core_g.at[3])
    for i, at in enumerate(parts):
        gx[1, i] = send(mine_g.at[1, :, :, at], fin_g.at[0, :, :, at], to_right)
        gx[3, i] = send(mine_g.at[3, :, :, at], fin_g.at[1, :, :, at], to_left)
    co[0].wait_recv()
    add(mine_o.at[0], core_o.at[0])
    cg[0].wait_recv()
    add(mine_g.at[0], core_g.at[0])

    for copy in locals_[:2]:
        copy.wait()
    tilt_row = lax.broadcasted_iota(jnp.int32, (TILTS, 1), 0)
    number = jnp.zeros((TILTS, 1), f32)
    for dt in range(4):
        number = jnp.where(tilt_row == dt, defocus[(X + dt) % 4, gz].astype(f32), number)
    frequency = line[0:1, :]
    phase = math.pi * wavelength * number * frequency * frequency
    response[...] = (
        -(amplitude_root * jnp.sin(phase) + contrast * jnp.cos(phase)) * line[1:2, :]
    )

    gcol = lax.broadcasted_iota(jnp.int32, (ROWS, 256), 1)
    grow = lax.broadcasted_iota(jnp.int32, (ROWS, 256), 0)
    zone = zl ^ ((gcol >> 4) & 1)
    place = 8 * (zone * 2 + (c ^ (gcol >> 7))) + (gcol & 7)
    place = place + ((gcol >> 3) & 1) * (32 - 64 * zone)
    tilt = (gcol >> 5) & 3
    there = place + xy * ROWS
    legal = (there >= 0) & (there < tiles * ROWS)
    back = []
    for z in range(LAYERS):
        s = jnp.zeros((ROWS, 256), jnp.int32)
        w = jnp.zeros((ROWS, 256), f32)
        for dt in range(4):
            s = jnp.where(tilt == dt, shift[dt, z], s)
            w = jnp.where(tilt == dt, far[dt, z], w)
        delta = place + s - grow
        both = jnp.where(delta == 0, 1.0 - w, 0.0) + jnp.where(delta == -1, w, 0.0)
        back.append(jnp.where(legal, both, 0.0))
    back_rows[...] = jnp.concatenate(back, 0).astype(bf16)

    gz_, waits = {}, []
    for i, at in enumerate(parts):
        for dt, slot, where in ((2, 2, to_far), (1, 0, to_right), (3, 1, to_left)):
            oz[dt, i].wait_recv()
            add(mine_o.at[0, dt, :, at], zin_o.at[dt, :, at])
            ox[dt, i] = send(mine_o.at[0, dt, :, at], fin_o.at[slot, :, at], where)
    for i, at in enumerate(parts):
        for dt in (2, 1, 3):
            gx[dt, i].wait_recv()
        mine_g[0, :, :, at] = (mine_g[0, :, :, at] + fin_g[0, :, :, at]) + (
            fin_g[1, :, :, at] + fin_g[2, :, :, at]
        )
        gz_[i] = send(mine_g.at[0, 1, :, at], zin_g.at[:, at], to_z)
    for i, at in enumerate(parts):
        oz[0, i].wait_recv()
        for dt in (2, 1, 3):
            ox[dt, i].wait_recv()
        mine_o[0, 0, :, at] = (
            (mine_o[0, 0, :, at] + zin_o[0, :, at])
            + (fin_o[0, :, at] + fin_o[1, :, at])
            + fin_o[2, :, at]
        )
        waits.append(
            send_halo(mine_o.at[0, 0, :, at], halo_o.at[:, at], to_behind, has_behind, has_ahead)
        )
        gz_[i].wait_recv()
        add(mine_g.at[0, 0, :, at], zin_g.at[:, at])
        waits.append(
            send_halo(mine_g.at[0, 0, :, at], halo_g.at[:, at], to_ahead, has_ahead, has_behind)
        )
    for copy in locals_[2:]:
        copy.wait()

    meas_wait()
    for wait in waits:
        wait()
    ray_norm = float(TILTS * 16) ** (-0.5)
    own_sum = mine_o[0, 0] + jnp.where(has_behind, halo_g[...], 0.0)
    own_rows = meas_rows[0] - ray_norm * own_sum
    ghost_rows = meas_rows[1] - ray_norm * (mine_g[0, 0] + halo_o[...])
    ghost_rows = jnp.where(has_ahead, ghost_rows, 0.0)
    residual = jnp.concatenate([own_rows, ghost_rows], 0)

    x = [residual[:, PART * a : PART * (a + 1)] for a in range(8)]
    root = math.sqrt(0.5)
    s04, d04 = x[0] + x[4], x[0] - x[4]
    s26, d26 = x[2] + x[6], x[2] - x[6]
    s15, d15 = x[1] + x[5], x[1] - x[5]
    s37, d37 = x[3] + x[7], x[3] - x[7]
    even, odd = s04 + s26, s15 + s37
    m = root * (d15 - d37)
    n = root * (d15 + d37)
    inputs = {
        0: even + odd,
        4: even - odd,
        1: jnp.concatenate([d04 + m, -(d26 + n)], 1),
        2: jnp.concatenate([s04 - s26, s37 - s15], 1),
        3: jnp.concatenate([d04 - m, d26 - n], 1),
    }
    for first, width, residue in GROUPS:
        high, low = split(inputs[residue])
        if width == 512:
            th, tl = fwd_big[0, residue - 1], fwd_big[1, residue - 1]
        else:
            th, tl = fwd_small[0, residue // 4], fwd_small[1, residue // 4]
        both = dot(jnp.concatenate([high, low], 0), th)
        lines = both[0:16] + both[16:32] + dot(high, tl)
        gathered[0, 0, 0, :, :, first : first + width] = lines.reshape(2, 8, width)

    half = (pl.ds(0, LINE // 2), pl.ds(LINE // 2, LINE // 2))

    def block(dt, dzl, ghost):
        return gathered.at[0, dt, dzl, ghost]

    def to_sides(dzl, ghost):
        src = block(0, dzl, ghost)
        return {
            3: send(src, block(3, dzl, ghost), to_right),
            1: send(src, block(1, dzl, ghost), to_left),
        }

    def pass_on(dt, dzl, ghost):
        at, where = (half[0], to_right) if dt == 3 else (half[1], to_left)
        src = gathered.at[0, dt, dzl, ghost, :, at]
        return send(src, gathered.at[0, 2, dzl, ghost, :, at], where)

    def along_z(dt, ghost):
        return send(block(dt, 0, ghost), block(dt, 1, ghost), to_z)

    passed = {}

    def to_other(dt, dzl, ghost):
        src = block(dt, dzl, ghost)
        passed.setdefault((dt, dzl), []).append(
            send(src, gathered.at[1, dt, dzl, ghost], to_core)
        )

    def scale(core, dt, dzl):
        lines = gathered[core, dt, dzl].reshape(16, LINE) * response[dt : dt + 1, :]
        high, low = split(lines)
        first = 256 * core + 32 * dt + 16 * dzl
        terms[first : first + 16, :] = high
        terms[first + 128 : first + 144, :] = low

    def combine(core):
        w = back_rows[:, 128 * core : 128 * core + 128]
        w = jnp.concatenate([w, w], 1)
        for at in quarter:
            u = dot(w, terms[256 * core : 256 * core + 256, at])
            spectral[:, at] = spectral[:, at] + u if core else u

    bx = to_sides(0, 0)
    az = along_z(0, 1)
    bx[2] = send(block(0, 0, 0), block(2, 0, 0), to_far)
    bz = {0: along_z(0, 0)}
    cx = to_sides(0, 1)
    to_other(0, 0, 0)
    to_other(0, 0, 1)
    for dt in (3, 1):
        bx[dt].wait_recv()
        bz[dt] = along_z(dt, 0)
    az.wait_recv()
    cz = {2: send(block(0, 1, 1), block(2, 1, 1), to_far)}
    cz.update(to_sides(1, 1))
    to_other(0, 1, 1)
    to_other(3, 0, 0)
    to_other(1, 0, 0)
    bz[0].wait_recv()
    to_other(0, 1, 0)
    scale(0, 0, 0)
    bx[2].wait_recv()
    bz[2] = along_z(2, 0)
    cfar = []
    for dt in (3, 1):
        cx[dt].wait_recv()
        cfar.append(pass_on(dt, 0, 1))
    to_other(2, 0, 0)
    to_other(3, 0, 1)
    to_other(1, 0, 1)
    scale(0, 0, 1)
    for dt in (3, 1):
        scale(0, dt, 0)
    bz[3].wait_recv()
    to_other(3, 1, 0)
    for copy in passed[0, 0]:
        copy.wait_recv()
    scale(1, 0, 0)
    bz[1].wait_recv()
    to_other(1, 1, 0)
    for dt in (2, 3, 1):
        cz[dt].wait_recv()
        to_other(dt, 1, 1)
    for copy in cfar:
        copy.wait_recv()
    to_other(2, 0, 1)
    scale(0, 2, 0)
    scale(0, 3, 1)
    scale(0, 1, 1)
    bz[2].wait_recv()
    to_other(2, 1, 0)
    scale(0, 2, 1)
    combine(0)
    for key in ((0, 1), (3, 0), (1, 0), (3, 1), (1, 1), (2, 0), (2, 1)):
        for copy in passed[key]:
            copy.wait_recv()
        scale(1, *key)
    combine(1)

    for first, width, residue in GROUPS:
        at = pl.ds(first, width)
        high, low = split(spectral[:, at])
        if width == 512:
            th, tl = inv_big[0, residue - 1], inv_big[1, residue - 1]
        else:
            th, tl = inv_small[0, residue // 4], inv_small[1, residue // 4]
        spectral[:, at] = dot(high, th) + dot(low, th) + dot(high, tl)

    def part(first):
        return spectral[:, first : first + PART]

    g0, g4 = part(0), part(256)
    r1, i1, r2, i2, r3, i3 = (part(512 + PART * i) for i in range(6))
    p, q = g0 + g4, g0 - g4
    pr, ps = p + r2, p - r2
    qm, qp = q - i2, q + i2
    r13, i31 = r1 + r3, i3 - i1
    rd, im = r1 - r3, i1 + i3
    v, w = root * (rd - im), root * (rd + im)
    ys = (pr + r13, qm + v, ps + i31, qp - w, pr - r13, qm - v, ps - i31, qp + w)
    for a in range(8):
        at = pl.ds(PART * a, PART)
        out[:, :, at] = vol[:, :, at] + ys[a].reshape(LAYERS, ROWS, PART)

    for copy in sent:
        copy.wait_send()
    for copy, there in halos:
        pl.when(there)(copy.wait_send)


def body(tiles, tables, volume, measured, ray_offset, defocus):
    fwd_big, fwd_small, inv_big, inv_small, line = tables
    hbm = pl.BlockSpec(memory_space=pltpu.HBM)

    def f(*shape):
        return pltpu.VMEM(shape, f32)

    arrays = (ray_offset, defocus, volume, measured, line, fwd_big, fwd_small, inv_big, inv_small)
    return pl.pallas_call(
        functools.partial(kernel, tiles),
        out_shape=pltpu.VMEM(volume.shape, f32),
        in_specs=[hbm] * 9,
        out_specs=pl.BlockSpec(memory_space=pltpu.VMEM),
        scratch_shapes=[
            pltpu.SMEM(ray_offset.shape, jnp.int32),
            pltpu.SMEM(defocus.shape, jnp.int32),
            f(*volume.shape),
            f(*line.shape),
            f(TILTS, LINE),
            pltpu.VMEM((128, 256), bf16),
            pltpu.VMEM(fwd_big.shape, bf16),
            pltpu.VMEM(fwd_small.shape, bf16),
            pltpu.VMEM(inv_big.shape, bf16),
            pltpu.VMEM(inv_small.shape, bf16),
            f(2, 8, LINE),
            pltpu.VMEM((256, LINE), bf16),
            f(4, 2, 8, LINE),
            f(2, 4, 8, LINE),
            f(4, 2, 8, LINE),
            f(2, 4, 8, LINE),
            f(4, 2, 8, LINE),
            f(2, 4, 8, LINE),
            f(3, 2, 8, LINE),
            f(8, LINE),
            f(4, 8, LINE),
            f(3, 8, LINE),
            f(8, LINE),
            f(8, LINE),
            f(2, 4, 2, 2, 8, LINE),
            f(128, LINE),
            pltpu.VMEM((512, LINE), bf16),
            pltpu.SemaphoreType.DMA((12,)),
            pltpu.SemaphoreType.DMA((SEMAPHORES,)),
            pltpu.SemaphoreType.DMA((SEMAPHORES,)),
        ],
        compiler_params=pltpu.CompilerParams(
            collective_id=0, has_side_effects=True, vmem_limit_bytes=40 * 1024 * 1024
        ),
        name="step",
    )(*(pltpu.with_memory_space_constraint(a, pltpu.HBM) for a in arrays))


def solution(mesh):
    placed = (P("gz", "xy", None), P(None, "xy", None), P(), P())
    tables = tuple(dft_tables())
    return jax.shard_map(
        functools.partial(body, mesh.shape["xy"], tables),
        mesh=mesh,
        in_specs=placed,
        out_specs=P("gz", "xy", None),
        check_vma=False,
    )
```

```python
import functools
import math

import jax
import jax.numpy as jnp
import ml_dtypes
import numpy as np
from jax import lax
from jax.experimental import pallas as pl
from jax.experimental.pallas import tpu as pltpu
from jax.sharding import PartitionSpec as P

HALO = 16
LINE = 2048
PART = 256
ROWS = 32
LAYERS = 4
TILTS = 4
SUM_PARTS = 2
SEMAPHORES = 64

pixel_size = 4.0
wavelength = 0.0197
contrast = 0.07
amplitude_root = math.sqrt(1.0 - 0.07 * 0.07)
f32 = jnp.float32
bf16 = jnp.bfloat16
MESH = pl.DeviceIdType.MESH

GROUPS = ((0, 256, 0), (256, 256, 4), (512, 512, 1), (1024, 512, 2), (1536, 512, 3))


def halves(table):
    high = table.astype(ml_dtypes.bfloat16)
    low = (table - high.astype(np.float64)).astype(ml_dtypes.bfloat16)
    return np.stack([high, low])


def dft_tables():
    b = np.arange(PART, dtype=np.int64)[:, None]
    tables, freq, scale = {}, [], []
    for _, width, residue in GROUPS:
        if residue == 0:
            re, im = np.arange(0, 129), np.arange(1, 128)
        elif residue == 4:
            re = im = np.arange(0, 128)
        else:
            re = im = np.arange(0, 256)
        f_re, f_im = residue + 8 * re, residue + 8 * im
        turn_re = 2 * np.pi / LINE * (b * f_re % LINE)
        turn_im = 2 * np.pi / LINE * (b * f_im % LINE)
        real_in = np.concatenate([np.cos(turn_re), -np.sin(turn_im)], 1)
        if width == 512:
            imag_in = np.concatenate([np.sin(turn_re), np.cos(turn_im)], 1)
            real_in = np.concatenate([real_in, imag_in], 0)
        tables[residue] = real_in
        f = np.concatenate([f_re, f_im])
        folded = np.where(2 * f < LINE, f, f - LINE)
        freq.append(folded / (LINE * pixel_size))
        scale.append(np.where((f == 0) | (f == LINE // 2), 1.0, 2.0) / (LINE * TILTS))
    big = np.stack([tables[1], tables[2], tables[3]])
    small = np.stack([tables[0], tables[4]])
    line = np.stack([np.concatenate(freq), np.concatenate(scale)]).astype(np.float32)
    return (
        halves(big),
        halves(small),
        halves(big.transpose(0, 2, 1)),
        halves(small.transpose(0, 2, 1)),
        line,
    )


def split(x):
    high = x.astype(bf16)
    low = (x - high.astype(f32)).astype(bf16)
    return high, low


def dot(a, b):
    return jnp.dot(a, b, preferred_element_type=f32)


def kernel(
    tiles,
    ray_hbm,
    defocus_hbm,
    vol_hbm,
    meas,
    line_hbm,
    fwd_big_hbm,
    fwd_small_hbm,
    inv_big_hbm,
    inv_small_hbm,
    out,
    ray,
    defocus,
    vol,
    line,
    response,
    back_rows,
    fwd_big,
    fwd_small,
    inv_big,
    inv_small,
    meas_rows,
    vcat,
    other_g,
    other_o,
    mine_g,
    mine_o,
    core_g,
    core_o,
    fin_g,
    zin_g,
    zin_o,
    fin_o,
    halo_g,
    halo_o,
    gathered,
    spectral,
    terms,
    local_sem,
    ss,
    rs,
):
    gz = lax.axis_index("gz")
    xy = lax.axis_index("xy")
    X = gz // 4
    zl = (gz // 2) % 2
    c = gz % 2
    to_core = {"gz": gz + 1 - 2 * c}
    to_z = {"gz": gz + 2 - 4 * zl}
    to_right = {"gz": (gz + 4) % 16}
    to_left = {"gz": (gz + 12) % 16}
    to_far = {"gz": (gz + 8) % 16}
    step = 1 - 2 * zl
    has_ahead = (xy + step >= 0) & (xy + step < tiles)
    has_behind = (xy - step >= 0) & (xy - step < tiles)
    to_ahead = {"xy": (xy + step + tiles) % tiles}
    to_behind = {"xy": (xy - step + tiles) % tiles}
    partners = (to_core, to_z, to_right, to_left, to_far)
    barrier = pltpu.get_barrier_semaphore()

    def greet(partner):
        pl.semaphore_signal(barrier, inc=1, device_id=partner, device_id_type=MESH)

    for partner in partners:
        greet(partner)
    pl.when(has_ahead)(lambda: greet(to_ahead))
    pl.when(has_behind)(lambda: greet(to_behind))
    greetings = len(partners) + has_ahead.astype(jnp.int32) + has_behind.astype(jnp.int32)

    k_own = zl * 2 + c
    meas_hbm = meas.at[X, pl.ds(pl.multiple_of(8 * k_own, 8), 8)]
    quarter = [pl.ds(512 * j, 512) for j in range(4)]
    start_copies = [pltpu.make_async_copy(ray_hbm, ray, local_sem.at[5])] + [
        pltpu.make_async_copy(vol_hbm.at[:, :, quarter[j]], vol.at[:, :, quarter[j]], local_sem.at[8 + j])
        for j in range(4)
    ]
    for copy in start_copies:
        copy.start()

    @pl.when(jnp.logical_not(has_behind))
    def _():
        halo_g[...] = jnp.zeros_like(halo_g)

    @pl.when(jnp.logical_not(has_ahead))
    def _():
        halo_o[...] = jnp.zeros_like(halo_o)
        meas_rows[1] = jnp.zeros((8, LINE), f32)

    locals_ = [
        pltpu.make_async_copy(defocus_hbm, defocus, local_sem.at[7]),
        pltpu.make_async_copy(line_hbm, line, local_sem.at[6]),
        pltpu.make_async_copy(meas_hbm, meas_rows.at[0], local_sem.at[0]),
        pltpu.make_async_copy(fwd_big_hbm, fwd_big, local_sem.at[1]),
        pltpu.make_async_copy(fwd_small_hbm, fwd_small, local_sem.at[2]),
        pltpu.make_async_copy(inv_big_hbm, inv_big, local_sem.at[3]),
        pltpu.make_async_copy(inv_small_hbm, inv_small, local_sem.at[4]),
    ]
    count = [0]
    sent = []
    halos = []

    def send(src, dst, where):
        i = count[0]
        count[0] += 1
        copy = pltpu.make_async_remote_copy(
            src_ref=src, dst_ref=dst, send_sem=ss.at[i], recv_sem=rs.at[i],
            device_id=where, device_id_type=MESH,
        )
        copy.start()
        sent.append(copy)
        return copy

    start_copies[0].wait()
    def send_halo(src, dst, where, there, back):
        i = count[0]
        count[0] += 1
        copy = pltpu.make_async_remote_copy(
            src_ref=src, dst_ref=dst, send_sem=ss.at[i], recv_sem=rs.at[i],
            device_id=where, device_id_type=MESH,
        )
        pl.when(there)(copy.start)
        halos.append((copy, there))
        return lambda: pl.when(back)(copy.wait_recv)

    shift, far = {}, {}
    for dt in range(4):
        t = (X + dt) % 4
        for z in range(LAYERS):
            offset = ray[t, gz * LAYERS + z]
            shift[dt, z] = offset >> 3
            far[dt, z] = (offset & 7).astype(f32) * 0.125

    col = lax.broadcasted_iota(jnp.int32, (8, 128), 1)
    sub = lax.broadcasted_iota(jnp.int32, (8, 128), 0)
    layer = col // ROWS
    target, near_row, far_row = {}, {}, {}
    for dt in range(4):
        s = jnp.zeros((8, 128), jnp.int32)
        w = jnp.zeros((8, 128), f32)
        for z in range(LAYERS):
            s = jnp.where(layer == z, shift[dt, z], s)
            w = jnp.where(layer == z, far[dt, z], w)
        target[dt] = col % ROWS - s
        near_row[dt], far_row[dt] = 1.0 - w, w

    def first_ext(zone, core, ghost):
        base = 8 * (zone * 2 + core)
        if ghost:
            base = base + 32 - 64 * zone
        return base

    def weights(core, ghost, dt, dzl):
        zone = zl ^ dzl
        e = sub + first_ext(zone, core, ghost)
        return jnp.where(e == target[dt], near_row[dt], 0.0) + jnp.where(
            e == target[dt] - 1, far_row[dt], 0.0
        )

    def lhs(core):
        blocks = [weights(core, True, dt, dzl) for dt in range(4) for dzl in range(2)]
        blocks += [weights(core, False, dt, dzl) for dzl in range(2) for dt in range(4)]
        w = jnp.concatenate(blocks, 0).astype(bf16)
        return jnp.concatenate([w, w], 1)

    def project(core, to_g, to_o, fill=False):
        w = lhs(core)
        for j, at in enumerate(quarter):
            if fill:
                start_copies[1 + j].wait()
                high, low = split(vol[:, :, at].reshape(LAYERS * ROWS, 512))
                vcat[0:128, at] = high
                vcat[128:256, at] = low
            p = dot(w, vcat[:, at])
            to_g[:, :, :, at] = p[0:64].reshape(4, 2, 8, 512)
            to_o[:, :, :, at] = p[64:128].reshape(2, 4, 8, 512)

    project(1 - c, other_g, other_o, fill=True)
    pl.semaphore_wait(barrier, greetings)
    cg, co = {}, {}
    cg[2] = send(other_g.at[2], core_g.at[2], to_core)
    co[1] = send(other_o.at[1], core_o.at[1], to_core)
    cg[1] = send(other_g.at[1], core_g.at[1], to_core)
    cg[3] = send(other_g.at[3], core_g.at[3], to_core)
    co[0] = send(other_o.at[0], core_o.at[0], to_core)
    cg[0] = send(other_g.at[0], core_g.at[0], to_core)
    for copy in locals_:
        copy.start()
    meas_wait = send_halo(meas_hbm, meas_rows.at[1], to_behind, has_behind, has_ahead)
    project(c, mine_g, mine_o)

    def add(dst, src):
        dst[...] = dst[...] + src[...]

    width = LINE // SUM_PARTS
    parts = [pl.ds(width * i, width) for i in range(SUM_PARTS)]
    cg[2].wait_recv()
    add(mine_g.at[2], core_g.at[2])
    gx, ox, oz = {}, {}, {}
    for i, at in enumerate(parts):
        gx[2, i] = send(mine_g.at[2, :, :, at], fin_g.at[2, :, :, at], to_far)
    co[1].wait_recv()
    add(mine_o.at[1], core_o.at[1])
    for i, at in enumerate(parts):
        for dt in (2, 1, 3, 0):
            oz[dt, i] = send(mine_o.at[1, dt, :, at], zin_o.at[dt, :, at], to_z)
    cg[1].wait_recv()
    add(mine_g.at[1], core_g.at[1])
    cg[3].wait_recv()
    add(mine_g.at[3], core_g.at[3])
    for i, at in enumerate(parts):
        gx[1, i] = send(mine_g.at[1, :, :, at], fin_g.at[0, :, :, at], to_right)
        gx[3, i] = send(mine_g.at[3, :, :, at], fin_g.at[1, :, :, at], to_left)
    co[0].wait_recv()
    add(mine_o.at[0], core_o.at[0])
    cg[0].wait_recv()
    add(mine_g.at[0], core_g.at[0])

    for copy in locals_[:2]:
        copy.wait()
    tilt_row = lax.broadcasted_iota(jnp.int32, (TILTS, 1), 0)
    number = jnp.zeros((TILTS, 1), f32)
    for dt in range(4):
        number = jnp.where(tilt_row == dt, defocus[(X + dt) % 4, gz].astype(f32), number)
    frequency = line[0:1, :]
    phase = math.pi * wavelength * number * frequency * frequency
    response[...] = (
        -(amplitude_root * jnp.sin(phase) + contrast * jnp.cos(phase)) * line[1:2, :]
    )

    gcol = lax.broadcasted_iota(jnp.int32, (ROWS, 256), 1)
    grow = lax.broadcasted_iota(jnp.int32, (ROWS, 256), 0)
    zone = zl ^ ((gcol >> 4) & 1)
    place = 8 * (zone * 2 + (c ^ (gcol >> 7))) + (gcol & 7)
    place = place + ((gcol >> 3) & 1) * (32 - 64 * zone)
    tilt = (gcol >> 5) & 3
    there = place + xy * ROWS
    legal = (there >= 0) & (there < tiles * ROWS)
    back = []
    for z in range(LAYERS):
        s = jnp.zeros((ROWS, 256), jnp.int32)
        w = jnp.zeros((ROWS, 256), f32)
        for dt in range(4):
            s = jnp.where(tilt == dt, shift[dt, z], s)
            w = jnp.where(tilt == dt, far[dt, z], w)
        delta = place + s - grow
        both = jnp.where(delta == 0, 1.0 - w, 0.0) + jnp.where(delta == -1, w, 0.0)
        back.append(jnp.where(legal, both, 0.0))
    back_rows[...] = jnp.concatenate(back, 0).astype(bf16)

    gz_, waits = {}, []
    for i, at in enumerate(parts):
        for dt, slot, where in ((2, 2, to_far), (1, 0, to_right), (3, 1, to_left)):
            oz[dt, i].wait_recv()
            add(mine_o.at[0, dt, :, at], zin_o.at[dt, :, at])
            ox[dt, i] = send(mine_o.at[0, dt, :, at], fin_o.at[slot, :, at], where)
    for i, at in enumerate(parts):
        for dt in (2, 1, 3):
            gx[dt, i].wait_recv()
        mine_g[0, :, :, at] = (mine_g[0, :, :, at] + fin_g[0, :, :, at]) + (
            fin_g[1, :, :, at] + fin_g[2, :, :, at]
        )
        gz_[i] = send(mine_g.at[0, 1, :, at], zin_g.at[:, at], to_z)
    for i, at in enumerate(parts):
        oz[0, i].wait_recv()
        for dt in (2, 1, 3):
            ox[dt, i].wait_recv()
        mine_o[0, 0, :, at] = (
            (mine_o[0, 0, :, at] + zin_o[0, :, at])
            + (fin_o[0, :, at] + fin_o[1, :, at])
            + fin_o[2, :, at]
        )
        waits.append(
            send_halo(mine_o.at[0, 0, :, at], halo_o.at[:, at], to_behind, has_behind, has_ahead)
        )
        gz_[i].wait_recv()
        add(mine_g.at[0, 0, :, at], zin_g.at[:, at])
        waits.append(
            send_halo(mine_g.at[0, 0, :, at], halo_g.at[:, at], to_ahead, has_ahead, has_behind)
        )
    for copy in locals_[2:]:
        copy.wait()

    meas_wait()
    for wait in waits:
        wait()
    ray_norm = float(TILTS * 16) ** (-0.5)
    own_sum = mine_o[0, 0] + jnp.where(has_behind, halo_g[...], 0.0)
    own_rows = meas_rows[0] - ray_norm * own_sum
    ghost_rows = meas_rows[1] - ray_norm * (mine_g[0, 0] + halo_o[...])
    ghost_rows = jnp.where(has_ahead, ghost_rows, 0.0)
    residual = jnp.concatenate([own_rows, ghost_rows], 0)

    x = [residual[:, PART * a : PART * (a + 1)] for a in range(8)]
    root = math.sqrt(0.5)
    s04, d04 = x[0] + x[4], x[0] - x[4]
    s26, d26 = x[2] + x[6], x[2] - x[6]
    s15, d15 = x[1] + x[5], x[1] - x[5]
    s37, d37 = x[3] + x[7], x[3] - x[7]
    even, odd = s04 + s26, s15 + s37
    m = root * (d15 - d37)
    n = root * (d15 + d37)
    inputs = {
        0: even + odd,
        4: even - odd,
        1: jnp.concatenate([d04 + m, -(d26 + n)], 1),
        2: jnp.concatenate([s04 - s26, s37 - s15], 1),
        3: jnp.concatenate([d04 - m, d26 - n], 1),
    }
    for first, width, residue in GROUPS:
        high, low = split(inputs[residue])
        if width == 512:
            th, tl = fwd_big[0, residue - 1], fwd_big[1, residue - 1]
        else:
            th, tl = fwd_small[0, residue // 4], fwd_small[1, residue // 4]
        both = dot(jnp.concatenate([high, low], 0), th)
        lines = both[0:16] + both[16:32] + dot(high, tl)
        gathered[0, 0, 0, :, :, first : first + width] = lines.reshape(2, 8, width)

    half = (pl.ds(0, LINE // 2), pl.ds(LINE // 2, LINE // 2))

    def block(dt, dzl, ghost):
        return gathered.at[0, dt, dzl, ghost]

    def to_sides(dzl, ghost):
        src = block(0, dzl, ghost)
        return {
            3: send(src, block(3, dzl, ghost), to_right),
            1: send(src, block(1, dzl, ghost), to_left),
        }

    def pass_on(dt, dzl, ghost):
        at, where = (half[0], to_right) if dt == 3 else (half[1], to_left)
        src = gathered.at[0, dt, dzl, ghost, :, at]
        return send(src, gathered.at[0, 2, dzl, ghost, :, at], where)

    def along_z(dt, ghost):
        return send(block(dt, 0, ghost), block(dt, 1, ghost), to_z)

    passed = {}

    def to_other(dt, dzl, ghost):
        src = block(dt, dzl, ghost)
        passed.setdefault((dt, dzl), []).append(
            send(src, gathered.at[1, dt, dzl, ghost], to_core)
        )

    def scale(core, dt, dzl):
        lines = gathered[core, dt, dzl].reshape(16, LINE) * response[dt : dt + 1, :]
        high, low = split(lines)
        first = 256 * core + 32 * dt + 16 * dzl
        terms[first : first + 16, :] = high
        terms[first + 128 : first + 144, :] = low

    def combine(core):
        w = back_rows[:, 128 * core : 128 * core + 128]
        w = jnp.concatenate([w, w], 1)
        for at in quarter:
            u = dot(w, terms[256 * core : 256 * core + 256, at])
            spectral[:, at] = spectral[:, at] + u if core else u

    bx = to_sides(0, 0)
    az = along_z(0, 1)
    bx[2] = send(block(0, 0, 0), block(2, 0, 0), to_far)
    bz = {0: along_z(0, 0)}
    cx = to_sides(0, 1)
    to_other(0, 0, 0)
    to_other(0, 0, 1)
    for dt in (3, 1):
        bx[dt].wait_recv()
        bz[dt] = along_z(dt, 0)
    az.wait_recv()
    cz = {2: send(block(0, 1, 1), block(2, 1, 1), to_far)}
    cz.update(to_sides(1, 1))
    to_other(0, 1, 1)
    to_other(3, 0, 0)
    to_other(1, 0, 0)
    bz[0].wait_recv()
    to_other(0, 1, 0)
    scale(0, 0, 0)
    bx[2].wait_recv()
    bz[2] = along_z(2, 0)
    cfar = []
    for dt in (3, 1):
        cx[dt].wait_recv()
        cfar.append(pass_on(dt, 0, 1))
    to_other(2, 0, 0)
    to_other(3, 0, 1)
    to_other(1, 0, 1)
    scale(0, 0, 1)
    for dt in (3, 1):
        scale(0, dt, 0)
    bz[3].wait_recv()
    to_other(3, 1, 0)
    for copy in passed[0, 0]:
        copy.wait_recv()
    scale(1, 0, 0)
    bz[1].wait_recv()
    to_other(1, 1, 0)
    for dt in (2, 3, 1):
        cz[dt].wait_recv()
        to_other(dt, 1, 1)
    for copy in cfar:
        copy.wait_recv()
    to_other(2, 0, 1)
    scale(0, 2, 0)
    scale(0, 3, 1)
    scale(0, 1, 1)
    bz[2].wait_recv()
    to_other(2, 1, 0)
    scale(0, 2, 1)
    combine(0)
    for key in ((0, 1), (3, 0), (1, 0), (3, 1), (1, 1), (2, 0), (2, 1)):
        for copy in passed[key]:
            copy.wait_recv()
        scale(1, *key)
    combine(1)

    for first, width, residue in GROUPS:
        at = pl.ds(first, width)
        high, low = split(spectral[:, at])
        if width == 512:
            th, tl = inv_big[0, residue - 1], inv_big[1, residue - 1]
        else:
            th, tl = inv_small[0, residue // 4], inv_small[1, residue // 4]
        both = dot(jnp.concatenate([high, low], 0), th)
        spectral[:, at] = both[0:128] + both[128:256] + dot(high, tl)

    def part(first):
        return spectral[:, first : first + PART]

    g0, g4 = part(0), part(256)
    r1, i1, r2, i2, r3, i3 = (part(512 + PART * i) for i in range(6))
    p, q = g0 + g4, g0 - g4
    pr, ps = p + r2, p - r2
    qm, qp = q - i2, q + i2
    r13, i31 = r1 + r3, i3 - i1
    rd, im = r1 - r3, i1 + i3
    v, w = root * (rd - im), root * (rd + im)
    ys = (pr + r13, qm + v, ps + i31, qp - w, pr - r13, qm - v, ps - i31, qp + w)
    for a in range(8):
        at = pl.ds(PART * a, PART)
        out[:, :, at] = vol[:, :, at] + ys[a].reshape(LAYERS, ROWS, PART)

    for copy in sent:
        copy.wait_send()
    for copy, there in halos:
        pl.when(there)(copy.wait_send)


def body(tiles, tables, volume, measured, ray_offset, defocus):
    fwd_big, fwd_small, inv_big, inv_small, line = tables
    hbm = pl.BlockSpec(memory_space=pltpu.HBM)

    def f(*shape):
        return pltpu.VMEM(shape, f32)

    arrays = (ray_offset, defocus, volume, measured, line, fwd_big, fwd_small, inv_big, inv_small)
    return pl.pallas_call(
        functools.partial(kernel, tiles),
        out_shape=pltpu.VMEM(volume.shape, f32),
        in_specs=[hbm] * 9,
        out_specs=pl.BlockSpec(memory_space=pltpu.VMEM),
        scratch_shapes=[
            pltpu.SMEM(ray_offset.shape, jnp.int32),
            pltpu.SMEM(defocus.shape, jnp.int32),
            f(*volume.shape),
            f(*line.shape),
            f(TILTS, LINE),
            pltpu.VMEM((128, 256), bf16),
            pltpu.VMEM(fwd_big.shape, bf16),
            pltpu.VMEM(fwd_small.shape, bf16),
            pltpu.VMEM(inv_big.shape, bf16),
            pltpu.VMEM(inv_small.shape, bf16),
            f(2, 8, LINE),
            pltpu.VMEM((256, LINE), bf16),
            f(4, 2, 8, LINE),
            f(2, 4, 8, LINE),
            f(4, 2, 8, LINE),
            f(2, 4, 8, LINE),
            f(4, 2, 8, LINE),
            f(2, 4, 8, LINE),
            f(3, 2, 8, LINE),
            f(8, LINE),
            f(4, 8, LINE),
            f(3, 8, LINE),
            f(8, LINE),
            f(8, LINE),
            f(2, 4, 2, 2, 8, LINE),
            f(128, LINE),
            pltpu.VMEM((512, LINE), bf16),
            pltpu.SemaphoreType.DMA((12,)),
            pltpu.SemaphoreType.DMA((SEMAPHORES,)),
            pltpu.SemaphoreType.DMA((SEMAPHORES,)),
        ],
        compiler_params=pltpu.CompilerParams(
            collective_id=0, has_side_effects=True, vmem_limit_bytes=40 * 1024 * 1024
        ),
        name="step",
    )(*(pltpu.with_memory_space_constraint(a, pltpu.HBM) for a in arrays))


def solution(mesh):
    placed = (P("gz", "xy", None), P(None, "xy", None), P(), P())
    tables = tuple(dft_tables())
    return jax.shard_map(
        functools.partial(body, mesh.shape["xy"], tables),
        mesh=mesh,
        in_specs=placed,
        out_specs=P("gz", "xy", None),
        check_vma=False,
    )
```
